256 devices in a mesh: blk: 32 (over y_lo, z, core), grp: 8 (over x, y_hi).
Axes of the slice: x: 4, y: 4 (y_hi: 2, y_lo: 2; y = y_hi * 2 + y_lo), z: 8, core: 2. Of those that a mesh axis runs over, the one named last changes fastest.
Arguments:
- queries: bfloat16 [8192, 2048], P(('blk', 'grp')), may hold values from -6 to 6
- windows: int32 [512], P(('blk', 'grp')), may hold values from 0 to 28
- library: bfloat16 [12288, 2048], P(('blk', 'grp')), may hold values from -6 to 6
- bands: int32 [1536], P(('blk', 'grp')), may hold values from 0 to 31
- shifts: int32 [4], replicated, may hold values from -24 to 24
Outputs:
- scored: float32 [8192, 16], P(('blk', 'grp'))
The draws below stay inside these ranges and needn't reach their ends.
All inputs are finite; a program needn't handle non-finite values.
Results may differ from the reference program's by a relative error of at most 0.0003.
Values may be sent and summed in bfloat16 or wider, within the bound.
A program may use at most 128 MiB of HBM per device.

```python
import math
import jax
import jax.numpy as jnp
from jax import lax

BINS = 2048
NOFF = 4
TOPK = 16
MAXSHIFT = 24
QBLK = 16
LBLK = 8
NBANDS = 32
SPAN = 4
L_DEV = 48
QUERIES = 8192
LIB = 12288


def band_law(key):
    key = jax.random.fold_in(key, 101)
    count = LIB // LBLK
    last = count - 1
    places = jnp.arange(count, dtype=jnp.int32)
    base = NBANDS * places * places // (last * last)
    jitter = jax.random.randint(jax.random.fold_in(key, 11), (count,), -1, 2, dtype=jnp.int32)
    inner = ((places > 0) & (places < last)).astype(jnp.int32)
    return jnp.clip(base + jitter * inner, 0, NBANDS - 1).astype(jnp.int32)


def window_law(key):
    key = jax.random.fold_in(key, 202)
    values = NBANDS - SPAN + 1
    ranks = jnp.arange(values, dtype=jnp.int32)
    weights = (27720 // (ranks + 1)).astype(jnp.int32)
    cumulative = jnp.cumsum(weights).astype(jnp.int32)
    count = QUERIES // QBLK
    picks = jax.random.randint(jax.random.fold_in(key, 1), (count,), 0, cumulative[values - 1], dtype=jnp.int32)
    rank = jnp.sum((picks[:, None] >= cumulative[None, :]).astype(jnp.int32), axis=1).astype(jnp.int32)
    order = jax.random.permutation(jax.random.fold_in(key, 2), values).astype(jnp.int32)
    return order[rank].astype(jnp.int32)


def cluster_rows():
    return math.gcd(L_DEV, 16)


def cluster_choice(key, bands, windows):
    key = jax.random.fold_in(key, 303)
    rows = cluster_rows()
    per = rows // LBLK
    clusters = LIB // rows
    first = bands[::per].astype(jnp.int32)
    query_win = jnp.repeat(windows, QBLK).astype(jnp.int32)
    distance = jnp.abs(first[None, :] - query_win[:, None] - 1).astype(jnp.int32)
    noise = jax.random.randint(jax.random.fold_in(key, 1), (QUERIES, clusters), 0, 4096, dtype=jnp.int32)
    index = jnp.arange(clusters, dtype=jnp.int32)
    score = ((NBANDS + 1 - distance) * 4096 + noise) * clusters + index[None, :]
    pick = lax.top_k(score, 1)[1][:, 0].astype(jnp.int32)
    matched = jax.random.randint(jax.random.fold_in(key, 2), (QUERIES,), 0, 2, dtype=jnp.int32)
    return (pick, matched)


def peak_field(key, cluster_ids):
    key = jax.random.fold_in(key, 404)
    clusters = LIB // cluster_rows()
    peaks = max(4, BINS // 64)
    centres = jax.random.uniform(jax.random.fold_in(key, 1), (clusters, peaks), jnp.float32, 0.0, float(BINS))
    heights = jax.random.uniform(jax.random.fold_in(key, 2), (clusters, peaks), jnp.float32, 1.0, 2.4)
    signs = jax.random.randint(jax.random.fold_in(key, 3), (clusters, peaks), 0, 2, dtype=jnp.int32)
    heights = heights * (2.0 * signs.astype(jnp.float32) - 1.0)
    width = MAXSHIFT / 2.0
    position = jnp.arange(BINS, dtype=jnp.float32)
    row_centres = centres[cluster_ids]
    row_heights = heights[cluster_ids]
    field = jnp.zeros((cluster_ids.shape[0], BINS), jnp.float32)
    for index in range(peaks):
        offset = position[None, :] - row_centres[:, index:index + 1]
        field = field + row_heights[:, index:index + 1] * jnp.exp(-(offset * offset) / (2.0 * width * width))
    return field


def shared_profile(key):
    key = jax.random.fold_in(key, 505)
    phase = jax.random.uniform(key, (), jnp.float32, 0.0, 2.0 * math.pi)
    position = jnp.arange(BINS, dtype=jnp.float32)
    return 1.0 + 0.5 * jnp.sin(2.0 * math.pi * 3.0 * position / BINS + phase)


def draw_bands(key, part):
    return band_law(key)


def draw_windows(key, part):
    return window_law(key)


def draw_queries(key, part):
    bands = band_law(key)
    windows = window_law(key)
    pick, matched = cluster_choice(key, bands, windows)
    base = peak_field(key, pick)
    profile = shared_profile(key)
    key = jax.random.fold_in(key, 3)
    noise = jax.random.normal(jax.random.fold_in(key, 1), (QUERIES, BINS), jnp.float32)
    pull = jnp.exp(jax.random.uniform(jax.random.fold_in(key, 2), (QUERIES,), jnp.float32, math.log(0.1), math.log(0.3)))
    value = pull[:, None] * profile[None, :] + matched.astype(jnp.float32)[:, None] * base + noise
    return jnp.clip(value, -6.0, 6.0).astype(jnp.bfloat16)


def draw_library(key, part):
    rows = cluster_rows()
    ids = (jnp.arange(LIB, dtype=jnp.int32) // rows).astype(jnp.int32)
    base = peak_field(key, ids)
    profile = shared_profile(key)
    key = jax.random.fold_in(key, 5)
    noise = jax.random.normal(jax.random.fold_in(key, 1), (LIB, BINS), jnp.float32)
    pull = jax.random.uniform(jax.random.fold_in(key, 2), (LIB,), jnp.float32, 0.6, 1.0)
    value = base - pull[:, None] * profile[None, :] + 0.5 * noise
    return jnp.clip(value, -6.0, 6.0).astype(jnp.bfloat16)


def with_ends(entries, own_key, least, largest):
    place = [jax.random.randint(jax.random.fold_in(own_key, axis), (), 0, length) for axis, length in enumerate(entries.shape)]
    longest = entries.shape.index(max(entries.shape))
    neighbour = place[:longest] + [(place[longest] + 1) % entries.shape[longest]] + place[longest + 1:]
    return entries.at[tuple(place)].set(least).at[tuple(neighbour)].set(largest)


def setup_inputs(seed: int = 0) -> dict:
    seeds = jax.random.split(jax.random.key(seed), 6)
    return {
        "queries": draw_queries(jax.random.fold_in(seeds[5], 71), 0),
        "windows": draw_windows(jax.random.fold_in(seeds[5], 71), 0),
        "library": draw_library(jax.random.fold_in(seeds[5], 71), 0),
        "bands": draw_bands(jax.random.fold_in(seeds[5], 71), 0),
        "shifts": with_ends(jax.random.randint(seeds[4], (NOFF,), -MAXSHIFT, MAXSHIFT + 1), jax.random.fold_in(seeds[4], 1), -MAXSHIFT, MAXSHIFT).astype(jnp.int32),
    }


EPS = 1e-06
MASKED = -8.0

def reference(queries, windows, library, bands, shifts):
    lib_wide = library.astype(jnp.float32)
    lib_scale = lax.rsqrt(lax.optimization_barrier(jnp.mean(lib_wide * lib_wide, axis=1)) + EPS)
    row_band = jnp.repeat(bands, LBLK)
    inv_root = 1.0 / math.sqrt(BINS)
    block = math.gcd(QUERIES, 256)
    query_win = jnp.repeat(windows, QBLK)
    grouped = queries.reshape(QUERIES // block, block, BINS)
    grouped_win = query_win.reshape(QUERIES // block, block)

    def score_block(pair):
        query_rows, lower = pair
        query_wide = query_rows.astype(jnp.float32)
        query_scale = lax.rsqrt(lax.optimization_barrier(jnp.mean(query_wide * query_wide, axis=1)) + EPS)
        padded = jnp.pad(query_wide, ((0, 0), (MAXSHIFT, MAXSHIFT)))
        best = None
        for index in range(NOFF):
            start = (MAXSHIFT + shifts[index]).astype(jnp.int32)
            moved = lax.dynamic_slice_in_dim(padded, start, BINS, 1)
            product = jnp.dot(moved, lib_wide.T, precision=lax.Precision.HIGHEST, preferred_element_type=jnp.float32)
            best = product if best is None else jnp.maximum(best, product)
        score = best * query_scale[:, None] * lib_scale[None, :] * inv_root
        inside = (row_band[None, :] >= lower[:, None]) & (row_band[None, :] < lower[:, None] + SPAN)
        score = jnp.where(inside, score, MASKED)
        return lax.top_k(score, TOPK)[0]
    result = lax.map(score_block, (grouped, grouped_win))
    return result.reshape(QUERIES, TOPK)
```

```python
import functools
import math

import jax
import jax.numpy as jnp
from jax import lax
from jax.experimental import pallas as pl
from jax.experimental.pallas import tpu as pltpu
from jax.sharding import PartitionSpec as P

BINS = 2048
NOFF = 4
TOPK = 16
MAXSHIFT = 24
QBLK = 16
LBLK = 8
SPAN = 4
EPS = 1e-06
MASKED = -8.0

QD = 32
LD = 48
CH = 16
NQ = 16 * QD
NL = 16 * LD
PAD = BINS + 2 * MAXSHIFT
MESH = pl.DeviceIdType.MESH

SLOTS = [
    (0, 0), (1, 0), (3, 0), (2, 0),
    (0, 1), (0, 3), (1, 1), (1, 3),
    (3, 1), (3, 3), (2, 1), (2, 3),
    (0, 2), (1, 2), (3, 2), (2, 2),
]


def qslot(a, b):
    return SLOTS.index((a % 4, b % 4))


def lplace(dz, c):
    dz %= 8
    if dz == 0:
        return c
    if dz == 4:
        return 14 + c
    d = min(dz, 8 - dz)
    return 2 + 4 * (d - 1) + 2 * c + (1 if dz > 4 else 0)


def batcher(n):
    pairs = []
    p = 1
    while p < n:
        k = p
        while k >= 1:
            for j in range(k % p, n - k, 2 * k):
                for i in range(min(k, n - j - k)):
                    if (i + j) // (2 * p) == (i + j + k) // (2 * p):
                        pairs.append((i + j, i + j + k))
            k //= 2
        p *= 2
    return pairs


SORT16 = batcher(16)


def sort16(v):
    v = list(v)
    for i, j in SORT16:
        v[i], v[j] = jnp.maximum(v[i], v[j]), jnp.minimum(v[i], v[j])
    return v


def merge16(a, b):
    v = [jnp.maximum(a[i], b[15 - i]) for i in range(16)]
    for d in (8, 4, 2, 1):
        for i in range(16):
            if not i & d:
                v[i], v[i + d] = jnp.maximum(v[i], v[i + d]), jnp.minimum(v[i], v[i + d])
    return v


def kernel(
    q_in, w_in, l_in, b_in, s_in, out,
    qbuf, lbuf, qt32, qtk, sc, lsc, lband, qrow, best, lmeta, qmeta, fin, got,
    loc_sem, qs_sem, qr_sem, ls_sem, lr_sem, ss_sem, sr_sem, m_sem, f_sem,
):
    blk = lax.axis_index("blk")
    grp = lax.axis_index("grp")
    core = lax.rem(blk, 2)
    z = lax.rem(lax.div(blk, 2), 8)
    x = lax.div(grp, 2)
    y = lax.rem(grp, 2) * 2 + lax.div(blk, 16)

    def place(px, py, pz, pc):
        return {
            "blk": (lax.rem(py, 2) * 8 + pz) * 2 + pc,
            "grp": px * 2 + lax.div(py, 2),
        }

    def plane(a, b):
        dx = a * (1 - core) + b * core
        dy = b * (1 - core) + a * core
        return place(lax.rem(x + dx, 4), lax.rem(y + dy, 4), z, core)

    def column(dz, dc):
        return place(x, y, lax.rem(z + dz, 8), core + dc * (1 - 2 * core))

    barrier = pltpu.get_barrier_semaphore()
    peers_p = [(a % 4, b % 4) for a, b in SLOTS[1:]]
    peers_c = [(dz, dc) for dc in range(2) for dz in range(8) if (dz, dc) != (0, 0)]
    for a, b in peers_p:
        pl.semaphore_signal(barrier, inc=1, device_id=plane(a, b), device_id_type=MESH)
    for dz, dc in peers_c:
        pl.semaphore_signal(barrier, inc=1, device_id=column(dz, dc), device_id_type=MESH)
    loc_q = pltpu.make_async_copy(q_in, qbuf.at[pl.ds(0, QD)], loc_sem.at[0])
    loc_l = pltpu.make_async_copy(l_in, lbuf.at[pl.ds(0, LD)], loc_sem.at[1])
    loc_q.start()
    loc_l.start()
    pl.semaphore_wait(barrier, 30)

    sends = []

    def lrows(dz, chunk):
        return lbuf.at[pl.ds(LD * lplace(dz, 0) + CH * chunk, CH)]

    def lsem(dz, chunk):
        return ((dz - 1) * 3) + chunk

    def l_send(src, dst_dz, chunk, step):
        n = lsem(dst_dz % 8, chunk)
        c = pltpu.make_async_remote_copy(
            src_ref=src, dst_ref=lrows(dst_dz, chunk), send_sem=ls_sem.at[n],
            recv_sem=lr_sem.at[n], device_id=column(step, 0), device_id_type=MESH,
        )
        c.start()
        sends.append(c)

    def l_wait(dz, chunk):
        n = lsem(dz % 8, chunk)
        ref = lrows(dz, chunk)
        pltpu.make_async_copy(ref, ref, lr_sem.at[n]).wait()

    def l_forward(d, chunk):
        l_wait(8 - d, chunk)
        l_wait(d, chunk)
        if d < 3:
            l_send(lrows(8 - d, chunk), 7 - d, chunk, 1)
            l_send(lrows(d, chunk), d + 1, chunk, 7)
        elif chunk == 0:
            l_send(lrows(5, 0), 4, 0, 1)
        elif chunk == 2:
            l_send(lrows(3, 2), 4, 2, 7)
        else:
            row = LD * (lplace(5, 0) * (1 - core) + lplace(3, 0) * core) + CH
            src = lbuf.at[pl.ds(pl.multiple_of(row, CH), CH)]
            l_send(src, 4, 1, 1 + 6 * core)

    def sib(src, dz):
        c = pltpu.make_async_remote_copy(
            src_ref=src, dst_ref=lbuf.at[pl.ds(LD * lplace(dz, 1), LD)],
            send_sem=ss_sem.at[dz], recv_sem=sr_sem.at[dz],
            device_id=column(0, 1), device_id_type=MESH,
        )
        c.start()
        sends.append(c)

    def sib_forward(dz):
        sib(lbuf.at[pl.ds(LD * lplace(dz, 0), LD)], dz)

    def sib_wait(dz):
        ref = lbuf.at[pl.ds(LD * lplace(dz, 1), LD)]
        pltpu.make_async_copy(ref, ref, sr_sem.at[dz]).wait()

    def qrows(a, b, half=None):
        s = QD * qslot(a, b)
        if half is None:
            return qbuf.at[pl.ds(s, QD)]
        return qbuf.at[pl.ds(s + 16 * half, 16)]

    def qsem(a, b, half):
        return qslot(a, b) * 2 + (half or 0)

    def q_send(src, a, b, half, to):
        n = qsem(a, b, half)
        c = pltpu.make_async_remote_copy(
            src_ref=src, dst_ref=qrows(a, b, half), send_sem=qs_sem.at[n],
            recv_sem=qr_sem.at[n], device_id=plane(*to), device_id_type=MESH,
        )
        c.start()
        sends.append(c)

    def q_wait(a, b, half=None):
        ref = qrows(a, b, half)
        pltpu.make_async_copy(ref, ref, qr_sem.at[qsem(a, b, half)]).wait()

    for chunk in range(3):
        src = l_in.at[pl.ds(CH * chunk, CH)]
        l_send(src, 7, chunk, 1)
        l_send(src, 1, chunk, 7)
        if chunk == 0:
            q_send(q_in, 3, 0, None, (1, 0))
            q_send(q_in, 1, 0, None, (3, 0))
            q_send(q_in, 0, 3, None, (0, 1))
            q_send(q_in, 0, 1, None, (0, 3))
    sib(l_in, 0)

    lane = lax.broadcasted_iota(jnp.int32, (1, 128), 1)

    def squares(ref, rows):
        acc = jnp.zeros((rows, 128), jnp.float32)
        for t in range(BINS // 128):
            v = ref[0:rows, 128 * t:128 * (t + 1)].astype(jnp.float32)
            acc = acc + v * v
        return acc

    def scale(total):
        return lax.rsqrt(jnp.sum(total.T, axis=0, keepdims=True) * (1.0 / BINS) + EPS)

    loc_q.wait()
    acc = squares(qbuf, QD)
    qscale = scale(jnp.concatenate([acc] * 4, axis=0)) * (1.0 / math.sqrt(BINS))
    first = lax.rem(lane, QD) < QBLK
    qwin = jnp.where(first, w_in[0], w_in[1]).astype(jnp.float32)
    qmeta[0, 0:1, :] = qscale
    qmeta[0, 1:2, :] = qwin
    loc_l.wait()
    acc = squares(lbuf, LD)
    lscale = scale(jnp.concatenate([acc, jnp.zeros((128 - LD, 128), jnp.float32)], axis=0))
    row_band = jnp.zeros((1, 128), jnp.int32)
    for j in range(LD // LBLK):
        row_band = jnp.where(lane >= 64 + LBLK * j, b_in[j], row_band)
    lmeta[0] = jnp.where(lane < 64, lscale, row_band.astype(jnp.float32))

    for a, b in peers_p:
        pltpu.make_async_remote_copy(
            src_ref=qmeta.at[0], dst_ref=qmeta.at[qslot(-a, -b)], send_sem=m_sem.at[0],
            recv_sem=m_sem.at[1], device_id=plane(a, b), device_id_type=MESH,
        ).start()
    for dz, dc in peers_c:
        pltpu.make_async_remote_copy(
            src_ref=lmeta.at[0], dst_ref=lmeta.at[lplace(-dz, dc)], send_sem=m_sem.at[2],
            recv_sem=m_sem.at[3], device_id=column(dz, dc), device_id_type=MESH,
        ).start()

    qt32[:, 0:MAXSHIFT, :] = jnp.zeros((4, MAXSHIFT, 128), jnp.float32)
    qt32[:, BINS + MAXSHIFT:PAD, :] = jnp.zeros((4, MAXSHIFT, 128), jnp.float32)
    best[...] = jnp.full(best.shape, -jnp.inf, jnp.float32)

    eye_r = lax.broadcasted_iota(jnp.int32, (256, 256), 0)
    eye_c = lax.broadcasted_iota(jnp.int32, (256, 256), 1)
    eye = (eye_r == eye_c).astype(jnp.float32).astype(jnp.bfloat16)

    def prepare(h):
        @pl.loop(0, BINS // 256)
        def _(i):
            c0 = pl.multiple_of(i * 256, 256)
            t = lax.dot_general(
                eye, qbuf[256 * h:256 * h + 256, pl.ds(c0, 256)],
                (((1,), (1,)), ((), ())), preferred_element_type=jnp.float32,
            )
            r0 = pl.multiple_of(MAXSHIFT + c0, 8)
            qt32[2 * h, pl.ds(r0, 256), :] = t[:, 0:128]
            qt32[2 * h + 1, pl.ds(r0, 256), :] = t[:, 128:256]

        for k in range(NOFF):
            off = s_in[k] + MAXSHIFT

            @pl.loop(0, BINS // 128)
            def _(i):
                r0 = pl.multiple_of(i * 128, 128)
                for t in range(2):
                    v = qt32[2 * h + t, pl.ds(r0 + off, 128), :]
                    c0 = 256 * h + 128 * t
                    qtk[k, pl.ds(r0, 128), c0:c0 + 128] = v.astype(jnp.bfloat16)

    def multiply(row, rows, h):
        cols = slice(256 * h, 256 * h + 256)
        for k in range(NOFF):
            d = jnp.dot(
                lbuf[row:row + rows, :], qtk[k, :, cols], preferred_element_type=jnp.float32
            )
            if k:
                d = jnp.maximum(sc[row:row + rows, cols], d)
            sc[row:row + rows, cols] = d

    def select(g0, g1):
        @pl.loop(g0, g1)
        def _(g):
            for t in range(4):
                cols = slice(128 * t, 128 * t + 128)
                scale_q = jnp.broadcast_to(qrow[0:1, cols], (8, 128))
                low = jnp.broadcast_to(qrow[1:2, cols], (8, 128))
                high = low + float(SPAN)
                vals = []
                for i in range(16):
                    r = pl.multiple_of(g * 128 + 8 * i, 8)
                    band = lband[pl.ds(r, 8), :]
                    v = sc[pl.ds(r, 8), cols] * scale_q * lsc[pl.ds(r, 8), :]
                    keep = (band >= low) & (band < high)
                    vals.append(jnp.where(keep, v, MASKED))
                vals = sort16(vals)
                vals = merge16([best[t, i] for i in range(16)], vals)
                for i in range(16):
                    best[t, i] = vals[i]

    l_forward(1, 0)
    q_wait(1, 0)
    q_wait(3, 0)
    q_send(qrows(1, 0, 1), 2, 0, 1, (3, 0))
    q_send(qrows(3, 0, 0), 2, 0, 0, (1, 0))
    for a in (1, 3):
        q_send(qrows(a, 0), a, 3, None, (0, 1))
        q_send(qrows(a, 0), a, 1, None, (0, 3))
    l_forward(1, 1)

    def q_far(a):
        q_wait(a, 1)
        q_wait(a, 3)
        q_send(qrows(a, 1, 1), a, 2, 1, (0, 3))
        q_send(qrows(a, 3, 0), a, 2, 0, (0, 1))

    q_wait(2, 0, 0)
    q_wait(2, 0, 1)
    q_send(qrows(2, 0), 2, 3, None, (0, 1))
    q_send(qrows(2, 0), 2, 1, None, (0, 3))
    q_far(0)
    l_forward(1, 2)
    sib_forward(1)
    sib_forward(7)
    q_far(1)
    l_forward(2, 0)
    prepare(0)
    l_forward(2, 1)
    q_far(3)
    for dz in (0, 1, 7):
        sib_wait(dz)
    multiply(0, 288, 0)
    l_forward(2, 2)
    sib_forward(2)
    sib_forward(6)
    q_far(2)

    pltpu.make_async_copy(lmeta.at[pl.ds(1, 15)], lmeta.at[pl.ds(1, 15)], m_sem.at[3]).wait()
    pltpu.make_async_copy(qmeta.at[pl.ds(1, 15)], qmeta.at[pl.ds(1, 15)], m_sem.at[1]).wait()

    @pl.loop(0, 16)
    def _(i):
        m = jnp.broadcast_to(lmeta[i], (128, 128)).T
        r = pl.multiple_of(i * LD, 8)
        lsc[pl.ds(r, LD), :] = m[0:LD]
        lband[pl.ds(r, LD), :] = m[64:64 + LD]

    part = lax.div(lax.broadcasted_iota(jnp.int32, (2, 128), 1), QD)
    for t in range(4):
        m = qmeta[4 * t]
        for p in range(1, 4):
            m = jnp.where(part == p, qmeta[4 * t + p], m)
        qrow[0:2, 128 * t:128 * t + 128] = m

    l_forward(3, 0)
    sib_wait(2)
    sib_wait(6)
    multiply(288, 192, 0)
    for a in (0, 1, 3, 2):
        q_wait(a, 2, 0)
        q_wait(a, 2, 1)
    l_forward(3, 1)
    prepare(1)
    l_forward(3, 2)
    sib_forward(3)
    sib_forward(5)
    multiply(0, 288, 1)
    multiply(288, 192, 1)
    select(0, 3)
    for chunk in range(3):
        l_wait(4, chunk)
    sib_forward(4)
    sib_wait(3)
    sib_wait(5)
    for h in range(2):
        multiply(480, 192, h)
    select(3, 5)
    sib_wait(4)
    for h in range(2):
        multiply(672, 96, h)
    select(5, 6)

    for t in range(4):
        vals = [best[t, i] for i in range(16)]
        for sh in (4, 2, 1):
            vals = merge16(vals, [pltpu.roll(v, sh, 0) for v in vals])
        for i in range(16):
            fin[t, i:i + 1, :] = vals[i][0:1]
        for p in range(4):
            n = 4 * t + p
            if n == 0:
                continue
            a, b = SLOTS[n]
            pltpu.make_async_remote_copy(
                src_ref=fin.at[t], dst_ref=got.at[n], send_sem=f_sem.at[0],
                recv_sem=f_sem.at[1], device_id=plane(a, b), device_id_type=MESH,
            ).start()
    got[0] = fin[0]
    for c in sends:
        c.wait_send()
    pltpu.make_async_copy(qmeta.at[pl.ds(1, 15)], qmeta.at[pl.ds(1, 15)], m_sem.at[0]).wait()
    pltpu.make_async_copy(lmeta.at[pl.ds(1, 15)], lmeta.at[pl.ds(1, 15)], m_sem.at[2]).wait()
    pltpu.make_async_copy(got.at[pl.ds(1, 15)], got.at[pl.ds(1, 15)], f_sem.at[0]).wait()
    pltpu.make_async_copy(got.at[pl.ds(1, 15)], got.at[pl.ds(1, 15)], f_sem.at[1]).wait()

    part = lax.div(lax.broadcasted_iota(jnp.int32, (8, 128), 1), QD)
    vals = []
    for r in range(16):
        rows = []
        for t in range(4):
            v = got[4 * t, r:r + 1, :]
            for p in range(1, 4):
                v = jnp.where(part[0:1] == p, got[4 * t + p, r:r + 1, :], v)
            rows.append(v)
        vals.append(jnp.concatenate(rows + rows, axis=0))
    for sh in (2, 1):
        vals = merge16(vals, [pltpu.roll(v, sh, 0) for v in vals])
    for sh in (64, 32):
        vals = merge16(vals, [pltpu.roll(v, sh, 1) for v in vals])
    full = jnp.concatenate([v[0:1] for v in vals] + [jnp.zeros((112, 128), jnp.float32)], axis=0)
    out[...] = full.T[0:QD, 0:TOPK]


def local(queries, windows, library, bands, shifts):
    dma = pltpu.SemaphoreType.DMA
    f32, bf16 = jnp.float32, jnp.bfloat16
    hbm = pl.BlockSpec(memory_space=pl.ANY)
    smem = pl.BlockSpec(memory_space=pltpu.SMEM)
    return pl.pallas_call(
        kernel,
        out_shape=jax.ShapeDtypeStruct((QD, TOPK), f32),
        in_specs=[hbm, smem, hbm, smem, smem],
        out_specs=pl.BlockSpec(memory_space=pltpu.VMEM),
        scratch_shapes=[
            pltpu.VMEM((NQ, BINS), bf16),
            pltpu.VMEM((NL, BINS), bf16),
            pltpu.VMEM((4, PAD, 128), f32),
            pltpu.VMEM((NOFF, BINS, NQ), bf16),
            pltpu.VMEM((NL, NQ), f32),
            pltpu.VMEM((NL, 128), f32),
            pltpu.VMEM((NL, 128), f32),
            pltpu.VMEM((8, NQ), f32),
            pltpu.VMEM((4, 16, 8, 128), f32),
            pltpu.VMEM((16, 1, 128), f32),
            pltpu.VMEM((16, 2, 128), f32),
            pltpu.VMEM((4, 16, 128), f32),
            pltpu.VMEM((16, 16, 128), f32),
            dma((2,)), dma((32,)), dma((32,)), dma((21,)), dma((21,)),
            dma((8,)), dma((8,)), dma((4,)), dma((2,)),
        ],
        compiler_params=pltpu.CompilerParams(
            collective_id=0, has_side_effects=True, vmem_limit_bytes=48 * 2**20
        ),
        cost_estimate=pl.CostEstimate(
            flops=2 * NQ * NL * BINS * NOFF, bytes_accessed=2 * (QD + LD) * BINS, transcendentals=0
        ),
    )(queries, windows, library, bands, shifts)


def solution(mesh):
    return jax.shard_map(
        local,
        mesh=mesh,
        in_specs=(
            P(("blk", "grp"), None),
            P(("blk", "grp")),
            P(("blk", "grp"), None),
            P(("blk", "grp")),
            P(),
        ),
        out_specs=P(("blk", "grp"), None),
        check_vma=False,
    )
```

```python
import functools
import math

import jax
import jax.numpy as jnp
from jax import lax
from jax.experimental import pallas as pl
from jax.experimental.pallas import tpu as pltpu
from jax.sharding import PartitionSpec as P

BINS = 2048
NOFF = 4
TOPK = 16
MAXSHIFT = 24
QBLK = 16
LBLK = 8
SPAN = 4
EPS = 1e-06
MASKED = -8.0

QD = 32
LD = 48
CH = 16
NQ = 16 * QD
NL = 16 * LD
PAD = BINS + 2 * MAXSHIFT
WIDE = BINS + 128
MESH = pl.DeviceIdType.MESH

SLOTS = [
    (0, 0), (1, 0), (3, 0), (2, 0),
    (0, 1), (0, 3), (1, 1), (1, 3),
    (3, 1), (3, 3), (2, 1), (2, 3),
    (0, 2), (1, 2), (3, 2), (2, 2),
]


def qslot(a, b):
    return SLOTS.index((a % 4, b % 4))


def lplace(dz, c):
    dz %= 8
    if dz == 0:
        return c
    if dz == 4:
        return 14 + c
    d = min(dz, 8 - dz)
    return 2 + 4 * (d - 1) + 2 * c + (1 if dz > 4 else 0)


def batcher(n):
    pairs = []
    p = 1
    while p < n:
        k = p
        while k >= 1:
            for j in range(k % p, n - k, 2 * k):
                for i in range(min(k, n - j - k)):
                    if (i + j) // (2 * p) == (i + j + k) // (2 * p):
                        pairs.append((i + j, i + j + k))
            k //= 2
        p *= 2
    return pairs


SORT16 = batcher(16)


def sort16(v):
    v = list(v)
    for i, j in SORT16:
        v[i], v[j] = jnp.maximum(v[i], v[j]), jnp.minimum(v[i], v[j])
    return v


def merge16(a, b):
    v = [jnp.maximum(a[i], b[15 - i]) for i in range(16)]
    for d in (8, 4, 2, 1):
        for i in range(16):
            if not i & d:
                v[i], v[i + d] = jnp.maximum(v[i], v[i + d]), jnp.minimum(v[i], v[i + d])
    return v


def kernel(
    q_in, w_hbm, l_in, b_hbm, s_hbm, out,
    w_in, b_in, s_in, qbuf, lbuf, qt32, qtk, sc, lsc, lband, qrow, best, lmeta, fin, got,
    loc_sem, qs_sem, qr_sem, ls_sem, lr_sem, ss_sem, sr_sem, ms_sem, mr_sem, f_sem,
):
    blk = lax.axis_index("blk")
    grp = lax.axis_index("grp")
    core = lax.rem(blk, 2)
    z = lax.rem(lax.div(blk, 2), 8)
    x = lax.div(grp, 2)
    y = lax.rem(grp, 2) * 2 + lax.div(blk, 16)

    def place(px, py, pz, pc):
        return {
            "blk": (lax.rem(py, 2) * 8 + pz) * 2 + pc,
            "grp": px * 2 + lax.div(py, 2),
        }

    def plane(a, b):
        dx = a * (1 - core) + b * core
        dy = b * (1 - core) + a * core
        return place(lax.rem(x + dx, 4), lax.rem(y + dy, 4), z, core)

    def column(dz, dc):
        return place(x, y, lax.rem(z + dz, 8), core + dc * (1 - 2 * core))

    barrier = pltpu.get_barrier_semaphore()
    near = [plane(1, 0), plane(3, 0), plane(0, 1), plane(0, 3)]
    near += [column(1, 0), column(7, 0), column(0, 1)]
    for peer in near:
        pl.semaphore_signal(barrier, inc=1, device_id=peer, device_id_type=MESH)
    loc_q = pltpu.make_async_copy(q_in, qbuf.at[pl.ds(0, QD), pl.ds(0, BINS)], loc_sem.at[0])
    loc_l = pltpu.make_async_copy(l_in, lbuf.at[pl.ds(0, LD)], loc_sem.at[1])
    loc_q.start()
    loc_l.start()
    small = [
        pltpu.make_async_copy(src, dst, loc_sem.at[2 + i])
        for i, (src, dst) in enumerate(((w_hbm, w_in), (b_hbm, b_in), (s_hbm, s_in)))
    ]
    for c in small:
        c.start()
    pl.semaphore_wait(barrier, len(near))

    sends = []

    def lrows(dz, chunk):
        return lbuf.at[pl.ds(LD * lplace(dz, 0) + CH * chunk, CH)]

    def lsem(dz, chunk):
        return ((dz - 1) * 3) + chunk

    def l_send(src, dst_dz, chunk, step):
        n = lsem(dst_dz % 8, chunk)
        c = pltpu.make_async_remote_copy(
            src_ref=src, dst_ref=lrows(dst_dz, chunk), send_sem=ls_sem.at[n],
            recv_sem=lr_sem.at[n], device_id=column(step, 0), device_id_type=MESH,
        )
        c.start()
        sends.append(c)

    def l_wait(dz, chunk):
        n = lsem(dz % 8, chunk)
        ref = lrows(dz, chunk)
        pltpu.make_async_copy(ref, ref, lr_sem.at[n]).wait()

    def l_forward(d, n):
        l_wait(8 - d, n)
        l_wait(d, 2 - n)
        if d < 3:
            l_send(lrows(8 - d, n), 7 - d, n, 1)
            l_send(lrows(d, 2 - n), d + 1, 2 - n, 7)
        elif n == 0:
            l_send(lrows(5, 0), 4, 0, 1)
            l_send(lrows(3, 2), 4, 2, 7)

    def l_middle():
        row = LD * (lplace(5, 0) * (1 - core) + lplace(3, 0) * core) + CH
        src = lbuf.at[pl.ds(pl.multiple_of(row, CH), CH)]
        l_send(src, 4, 1, 1 + 6 * core)

    def m_send(src_dz, dst_dz, step):
        c = pltpu.make_async_remote_copy(
            src_ref=lmeta.at[src_dz], dst_ref=lmeta.at[dst_dz],
            send_sem=ms_sem.at[dst_dz], recv_sem=mr_sem.at[dst_dz],
            device_id=column(step, 0), device_id_type=MESH,
        )
        c.start()
        sends.append(c)

    def m_wait(dz):
        pltpu.make_async_copy(lmeta.at[dz], lmeta.at[dz], mr_sem.at[dz]).wait()

    def m_forward(d):
        m_wait(8 - d)
        m_wait(d)
        m_send(8 - d, 7 - d, 1)
        if d < 3:
            m_send(d, d + 1, 7)

    def sib(src, dz):
        c = pltpu.make_async_remote_copy(
            src_ref=src, dst_ref=lbuf.at[pl.ds(LD * lplace(dz, 1), LD)],
            send_sem=ss_sem.at[dz], recv_sem=sr_sem.at[dz],
            device_id=column(0, 1), device_id_type=MESH,
        )
        c.start()
        sends.append(c)

    def sib_forward(dz):
        sib(lbuf.at[pl.ds(LD * lplace(dz, 0), LD)], dz)

    def sib_wait(dz):
        ref = lbuf.at[pl.ds(LD * lplace(dz, 1), LD)]
        pltpu.make_async_copy(ref, ref, sr_sem.at[dz]).wait()

    def qrows(a, b, half=None):
        s = QD * qslot(a, b)
        if half is None:
            return qbuf.at[pl.ds(s, QD)]
        return qbuf.at[pl.ds(s + 16 * half, 16)]

    def qsem(a, b, half):
        return qslot(a, b) * 2 + (half or 0)

    def q_send(src, a, b, half, to):
        n = qsem(a, b, half)
        c = pltpu.make_async_remote_copy(
            src_ref=src, dst_ref=qrows(a, b, half), send_sem=qs_sem.at[n],
            recv_sem=qr_sem.at[n], device_id=plane(*to), device_id_type=MESH,
        )
        c.start()
        sends.append(c)

    def q_wait(a, b, half=None):
        ref = qrows(a, b, half)
        pltpu.make_async_copy(ref, ref, qr_sem.at[qsem(a, b, half)]).wait()

    for n in range(3):
        l_send(l_in.at[pl.ds(CH * n, CH)], 7, n, 1)
        l_send(l_in.at[pl.ds(CH * (2 - n), CH)], 1, 2 - n, 7)
    sib(l_in, 0)

    lane = lax.broadcasted_iota(jnp.int32, (1, 128), 1)

    def squares(ref, rows):
        acc = jnp.zeros((rows, 128), jnp.float32)
        for t in range(BINS // 128):
            v = ref[0:rows, 128 * t:128 * (t + 1)].astype(jnp.float32)
            acc = acc + v * v
        return acc

    for c in small:
        c.wait()
    loc_q.wait()
    total = jnp.sum(squares(qbuf, QD), axis=1, keepdims=True)
    qscale = lax.rsqrt(total * (1.0 / BINS) + EPS) * (1.0 / math.sqrt(BINS))
    high = qscale.astype(jnp.bfloat16).astype(jnp.float32)
    mid = (qscale - high).astype(jnp.bfloat16).astype(jnp.float32)
    rest = qscale - high - mid
    row = lax.broadcasted_iota(jnp.int32, (QD, 128), 0)
    col = lax.broadcasted_iota(jnp.int32, (QD, 128), 1)
    ext = jnp.where(row < QBLK, w_in[0], w_in[1]).astype(jnp.float32)
    for i, piece in enumerate((high, mid, rest)):
        ext = jnp.where(col == i + 1, piece, ext)
    qbuf[0:QD, BINS:WIDE] = ext.astype(jnp.bfloat16)
    q_send(qrows(0, 0), 3, 0, None, (1, 0))
    q_send(qrows(0, 0), 1, 0, None, (3, 0))

    loc_l.wait()
    acc = squares(lbuf, LD)
    acc = jnp.concatenate([acc, jnp.zeros((128 - LD, 128), jnp.float32)], axis=0)
    total = jnp.sum(acc.T, axis=0, keepdims=True)
    lscale = lax.rsqrt(total * (1.0 / BINS) + EPS)
    row_band = jnp.zeros((1, 128), jnp.int32)
    for j in range(LD // LBLK):
        row_band = jnp.where(lane >= 64 + LBLK * j, b_in[j], row_band)
    lmeta[0] = jnp.where(lane < 64, lscale, row_band.astype(jnp.float32))
    m_send(0, 7, 1)
    m_send(0, 1, 7)
    q_send(qrows(0, 0), 0, 3, None, (0, 1))
    q_send(qrows(0, 0), 0, 1, None, (0, 3))

    qt32[:, 0:MAXSHIFT, :] = jnp.zeros((4, MAXSHIFT, 128), jnp.float32)
    qt32[:, BINS + MAXSHIFT:PAD, :] = jnp.zeros((4, MAXSHIFT, 128), jnp.float32)
    best[...] = jnp.full(best.shape, -jnp.inf, jnp.float32)

    eye_r = lax.broadcasted_iota(jnp.int32, (256, 256), 0)
    eye_c = lax.broadcasted_iota(jnp.int32, (256, 256), 1)
    eye = (eye_r == eye_c).astype(jnp.float32).astype(jnp.bfloat16)

    def turned(t, c0, width):
        return lax.dot_general(
            eye[0:width, 0:width], qbuf[128 * t:128 * t + 128, pl.ds(c0, width)],
            (((1,), (1,)), ((), ())), preferred_element_type=jnp.float32,
        )

    def prepare(t):
        cols = slice(128 * t, 128 * t + 128)

        @pl.loop(0, BINS // 256)
        def _(i):
            c0 = pl.multiple_of(i * 256, 256)
            r0 = pl.multiple_of(MAXSHIFT + c0, 8)
            qt32[t, pl.ds(r0, 256), :] = turned(t, c0, 256)

        ext = turned(t, BINS, 128)
        qrow[0:1, cols] = ext[1:2] + ext[2:3] + ext[3:4]
        qrow[1:2, cols] = ext[0:1]
        for k in range(NOFF):
            off = s_in[k] + MAXSHIFT

            @pl.loop(0, BINS // 256)
            def _(i):
                r0 = pl.multiple_of(i * 256, 256)
                v = qt32[t, pl.ds(r0 + off, 256), :]
                qtk[k, pl.ds(r0, 256), cols] = v.astype(jnp.bfloat16)

    def multiply(row, rows, h):
        cols = slice(256 * h, 256 * h + 256)
        for k in range(NOFF):
            d = jnp.dot(
                lbuf[row:row + rows, :], qtk[k, :, cols], preferred_element_type=jnp.float32
            )
            if k:
                d = jnp.maximum(sc[row:row + rows, cols], d)
            sc[row:row + rows, cols] = d

    def select(g0, g1, tiles):
        @pl.loop(g0, g1)
        def _(g):
            for t in tiles:
                cols = slice(128 * t, 128 * t + 128)
                scale_q = jnp.broadcast_to(qrow[0:1, cols], (8, 128))
                low = jnp.broadcast_to(qrow[1:2, cols], (8, 128))
                high = low + float(SPAN)
                vals = []
                for i in range(16):
                    r = pl.multiple_of(g * 128 + 8 * i, 8)
                    band = lband[pl.ds(r, 8), :]
                    v = sc[pl.ds(r, 8), cols] * scale_q * lsc[pl.ds(r, 8), :]
                    keep = (band >= low) & (band < high)
                    vals.append(jnp.where(keep, v, MASKED))
                vals = sort16(vals)
                vals = merge16([best[t, i] for i in range(16)], vals)
                for i in range(16):
                    best[t, i] = vals[i]

    def q_far(a):
        q_wait(a, 1)
        q_wait(a, 3)
        q_send(qrows(a, 1, 1), a, 2, 1, (0, 3))
        q_send(qrows(a, 3, 0), a, 2, 0, (0, 1))

    l_forward(1, 0)
    q_wait(1, 0)
    q_wait(3, 0)
    q_send(qrows(1, 0, 1), 2, 0, 1, (3, 0))
    q_send(qrows(3, 0, 0), 2, 0, 0, (1, 0))
    for a in (1, 3):
        q_send(qrows(a, 0), a, 3, None, (0, 1))
        q_send(qrows(a, 0), a, 1, None, (0, 3))
    m_forward(1)
    l_forward(1, 1)
    q_far(0)
    q_wait(2, 0, 0)
    q_wait(2, 0, 1)
    q_send(qrows(2, 0), 2, 3, None, (0, 1))
    q_send(qrows(2, 0), 2, 1, None, (0, 3))
    prepare(0)
    m_forward(2)
    l_forward(1, 2)
    sib_forward(1)
    sib_forward(7)
    q_far(1)
    l_forward(2, 0)
    prepare(1)
    m_forward(3)
    for dz in (0, 1, 7):
        sib_wait(dz)
    multiply(0, 288, 0)
    l_forward(2, 1)
    q_far(3)
    q_far(2)
    l_forward(2, 2)
    sib_forward(2)
    sib_forward(6)

    m_wait(4)
    pltpu.make_async_remote_copy(
        src_ref=lmeta.at[pl.ds(0, 8)], dst_ref=lmeta.at[pl.ds(8, 8)], send_sem=ms_sem.at[0],
        recv_sem=mr_sem.at[0], device_id=column(0, 1), device_id_type=MESH,
    ).start()
    prepare(2)
    l_forward(3, 0)
    sib_wait(2)
    sib_wait(6)
    multiply(288, 192, 0)
    pltpu.make_async_copy(lmeta.at[pl.ds(8, 8)], lmeta.at[pl.ds(8, 8)], mr_sem.at[0]).wait()
    for c in range(2):
        for dz in range(8):
            m = jnp.broadcast_to(lmeta[8 * c + dz], (128, 128)).T
            r = LD * lplace(dz, c)
            lsc[r:r + LD, :] = m[0:LD]
            lband[r:r + LD, :] = m[64:64 + LD]
    l_wait(5, 1)
    l_wait(3, 1)
    l_middle()
    for a in (0, 1, 3, 2):
        q_wait(a, 2, 0)
        q_wait(a, 2, 1)
    prepare(3)
    multiply(0, 288, 1)
    l_wait(5, 2)
    l_wait(3, 0)
    sib_forward(3)
    sib_forward(5)
    multiply(288, 192, 1)
    for n in range(3):
        l_wait(4, n)
    sib_forward(4)
    select(0, 3, range(4))
    sib_wait(3)
    sib_wait(5)
    multiply(480, 192, 0)
    multiply(480, 192, 1)
    select(3, 5, range(4))
    sib_wait(4)

    def finish(t):
        vals = [best[t, i] for i in range(16)]
        for sh in (4, 2, 1):
            vals = merge16(vals, [pltpu.roll(v, sh, 0) for v in vals])
        for i in range(16):
            fin[t, i:i + 1, :] = vals[i][0:1]
        for p in (3, 2, 1, 0):
            n = 4 * t + p
            if n == 0:
                continue
            a, b = SLOTS[n]
            pltpu.make_async_remote_copy(
                src_ref=fin.at[t], dst_ref=got.at[n], send_sem=f_sem.at[0],
                recv_sem=f_sem.at[1], device_id=plane(a, b), device_id_type=MESH,
            ).start()

    for h in (1, 0):
        multiply(672, 96, h)
        for t in (2 * h + 1, 2 * h):
            select(5, 6, (t,))
            finish(t)
    got[0] = fin[0]
    for c in sends:
        c.wait_send()
    pltpu.make_async_copy(lmeta.at[pl.ds(0, 8)], lmeta.at[pl.ds(0, 8)], ms_sem.at[0]).wait()
    pltpu.make_async_copy(got.at[pl.ds(1, 15)], got.at[pl.ds(1, 15)], f_sem.at[0]).wait()
    pltpu.make_async_copy(got.at[pl.ds(1, 15)], got.at[pl.ds(1, 15)], f_sem.at[1]).wait()

    part = lax.div(lax.broadcasted_iota(jnp.int32, (8, 128), 1), QD)
    vals = []
    for r in range(16):
        rows = []
        for t in range(4):
            v = got[4 * t, r:r + 1, :]
            for p in range(1, 4):
                v = jnp.where(part[0:1] == p, got[4 * t + p, r:r + 1, :], v)
            rows.append(v)
        vals.append(jnp.concatenate(rows + rows, axis=0))
    for sh in (2, 1):
        vals = merge16(vals, [pltpu.roll(v, sh, 0) for v in vals])
    for sh in (64, 32):
        vals = merge16(vals, [pltpu.roll(v, sh, 1) for v in vals])
    for i in range(TOPK):
        out[i:i + 1, :] = vals[i][0:1, 0:QD]


def local(queries, windows, library, bands, shifts):
    dma = pltpu.SemaphoreType.DMA
    f32, bf16 = jnp.float32, jnp.bfloat16
    hbm = pl.BlockSpec(memory_space=pltpu.HBM)
    return pl.pallas_call(
        kernel,
        out_shape=jax.ShapeDtypeStruct((TOPK, QD), f32),
        in_specs=[hbm] * 5,
        out_specs=pl.BlockSpec(memory_space=pltpu.VMEM),
        scratch_shapes=[
            pltpu.SMEM((2,), jnp.int32),
            pltpu.SMEM((6,), jnp.int32),
            pltpu.SMEM((NOFF,), jnp.int32),
            pltpu.VMEM((NQ, WIDE), bf16),
            pltpu.VMEM((NL, BINS), bf16),
            pltpu.VMEM((4, PAD, 128), f32),
            pltpu.VMEM((NOFF, BINS, NQ), bf16),
            pltpu.VMEM((NL, NQ), f32),
            pltpu.VMEM((NL, 128), f32),
            pltpu.VMEM((NL, 128), f32),
            pltpu.VMEM((8, NQ), f32),
            pltpu.VMEM((4, 16, 8, 128), f32),
            pltpu.VMEM((16, 1, 128), f32),
            pltpu.VMEM((4, 16, 128), f32),
            pltpu.VMEM((16, 16, 128), f32),
            dma((5,)), dma((32,)), dma((32,)), dma((21,)), dma((21,)),
            dma((8,)), dma((8,)), dma((8,)), dma((8,)), dma((2,)),
        ],
        compiler_params=pltpu.CompilerParams(
            collective_id=0, has_side_effects=True, vmem_limit_bytes=62 * 2**20
        ),
        cost_estimate=pl.CostEstimate(
            flops=2 * NQ * NL * BINS * NOFF, bytes_accessed=2 * (QD + LD) * BINS, transcendentals=0
        ),
    )(queries, windows, library, bands, shifts).T


def solution(mesh):
    return jax.shard_map(
        local,
        mesh=mesh,
        in_specs=(
            P(("blk", "grp"), None),
            P(("blk", "grp")),
            P(("blk", "grp"), None),
            P(("blk", "grp")),
            P(),
        ),
        out_specs=P(("blk", "grp"), None),
        check_vma=False,
    )
```

```python
import functools
import math

import jax
import jax.numpy as jnp
from jax import lax
from jax.experimental import pallas as pl
from jax.experimental.pallas import tpu as pltpu
from jax.sharding import PartitionSpec as P

BINS = 2048
NOFF = 4
TOPK = 16
MAXSHIFT = 24
QBLK = 16
LBLK = 8
SPAN = 4
EPS = 1e-06
MASKED = -8.0

QD = 32
LD = 48
CH = 16
NQ = 16 * QD
NL = 16 * LD
PAD = BINS + 2 * MAXSHIFT
WIDE = BINS + 128
MESH = pl.DeviceIdType.MESH

SLOTS = [
    (0, 0), (1, 0), (3, 0), (2, 0),
    (0, 1), (0, 3), (1, 1), (1, 3),
    (3, 1), (3, 3), (2, 1), (2, 3),
    (0, 2), (1, 2), (3, 2), (2, 2),
]


def qslot(a, b):
    return SLOTS.index((a % 4, b % 4))


def lplace(dz, c):
    dz %= 8
    if dz == 0:
        return c
    if dz == 4:
        return 14 + c
    d = min(dz, 8 - dz)
    return 2 + 4 * (d - 1) + 2 * c + (1 if dz > 4 else 0)


def batcher(n):
    pairs = []
    p = 1
    while p < n:
        k = p
        while k >= 1:
            for j in range(k % p, n - k, 2 * k):
                for i in range(min(k, n - j - k)):
                    if (i + j) // (2 * p) == (i + j + k) // (2 * p):
                        pairs.append((i + j, i + j + k))
            k //= 2
        p *= 2
    return pairs


SORT16 = batcher(16)


def sort16(v):
    v = list(v)
    for i, j in SORT16:
        v[i], v[j] = jnp.maximum(v[i], v[j]), jnp.minimum(v[i], v[j])
    return v


def merge16(a, b):
    v = [jnp.maximum(a[i], b[15 - i]) for i in range(16)]
    for d in (8, 4, 2, 1):
        for i in range(16):
            if not i & d:
                v[i], v[i + d] = jnp.maximum(v[i], v[i + d]), jnp.minimum(v[i], v[i + d])
    return v


def kernel(
    q_in, w_hbm, l_in, b_hbm, s_hbm, out,
    w_in, b_in, s_in, qbuf, lbuf, qt32, qtk, sc, lsc, lband, qrow, best, lmeta, fin, got,
    loc_sem, qs_sem, qr_sem, ls_sem, lr_sem, ss_sem, sr_sem, ms_sem, mr_sem, f_sem,
):
    blk = lax.axis_index("blk")
    grp = lax.axis_index("grp")
    core = lax.rem(blk, 2)
    z = lax.rem(lax.div(blk, 2), 8)
    x = lax.div(grp, 2)
    y = lax.rem(grp, 2) * 2 + lax.div(blk, 16)

    def place(px, py, pz, pc):
        return {
            "blk": (lax.rem(py, 2) * 8 + pz) * 2 + pc,
            "grp": px * 2 + lax.div(py, 2),
        }

    def plane(a, b):
        dx = a * (1 - core) + b * core
        dy = b * (1 - core) + a * core
        return place(lax.rem(x + dx, 4), lax.rem(y + dy, 4), z, core)

    def column(dz, dc):
        return place(x, y, lax.rem(z + dz, 8), core + dc * (1 - 2 * core))

    barrier = pltpu.get_barrier_semaphore()
    near = [plane(1, 0), plane(3, 0), plane(0, 1), plane(0, 3)]
    near += [column(1, 0), column(7, 0), column(0, 1)]
    for peer in near:
        pl.semaphore_signal(barrier, inc=1, device_id=peer, device_id_type=MESH)
    loc_q = pltpu.make_async_copy(q_in, qbuf.at[pl.ds(0, QD), pl.ds(0, BINS)], loc_sem.at[0])
    loc_l = pltpu.make_async_copy(l_in, lbuf.at[pl.ds(0, LD)], loc_sem.at[1])
    loc_q.start()
    loc_l.start()
    small = [
        pltpu.make_async_copy(src, dst, loc_sem.at[2 + i])
        for i, (src, dst) in enumerate(((w_hbm, w_in), (b_hbm, b_in), (s_hbm, s_in)))
    ]
    for c in small:
        c.start()
    pl.semaphore_wait(barrier, len(near))

    sends = []

    def lrows(dz, chunk):
        return lbuf.at[pl.ds(LD * lplace(dz, 0) + CH * chunk, CH)]

    def lsem(dz, chunk):
        return ((dz - 1) * 3) + chunk

    def l_send(src, dst_dz, chunk, step):
        n = lsem(dst_dz % 8, chunk)
        c = pltpu.make_async_remote_copy(
            src_ref=src, dst_ref=lrows(dst_dz, chunk), send_sem=ls_sem.at[n],
            recv_sem=lr_sem.at[n], device_id=column(step, 0), device_id_type=MESH,
        )
        c.start()
        sends.append(c)

    def l_wait(dz, chunk):
        n = lsem(dz % 8, chunk)
        ref = lrows(dz, chunk)
        pltpu.make_async_copy(ref, ref, lr_sem.at[n]).wait()

    def l_forward(d, n):
        l_wait(8 - d, n)
        l_wait(d, 2 - n)
        if d < 3:
            l_send(lrows(8 - d, n), 7 - d, n, 1)
            l_send(lrows(d, 2 - n), d + 1, 2 - n, 7)
        elif n == 0:
            l_send(lrows(5, 0), 4, 0, 1)
            l_send(lrows(3, 2), 4, 2, 7)

    def l_middle():
        row = LD * (lplace(5, 0) * (1 - core) + lplace(3, 0) * core) + CH
        src = lbuf.at[pl.ds(pl.multiple_of(row, CH), CH)]
        l_send(src, 4, 1, 1 + 6 * core)

    def m_send(src_dz, dst_dz, step):
        c = pltpu.make_async_remote_copy(
            src_ref=lmeta.at[src_dz], dst_ref=lmeta.at[dst_dz],
            send_sem=ms_sem.at[dst_dz], recv_sem=mr_sem.at[dst_dz],
            device_id=column(step, 0), device_id_type=MESH,
        )
        c.start()
        sends.append(c)

    def m_wait(dz):
        pltpu.make_async_copy(lmeta.at[dz], lmeta.at[dz], mr_sem.at[dz]).wait()

    def m_forward(d):
        m_wait(8 - d)
        m_wait(d)
        m_send(8 - d, 7 - d, 1)
        if d < 3:
            m_send(d, d + 1, 7)

    def sib(src, dz):
        c = pltpu.make_async_remote_copy(
            src_ref=src, dst_ref=lbuf.at[pl.ds(LD * lplace(dz, 1), LD)],
            send_sem=ss_sem.at[dz], recv_sem=sr_sem.at[dz],
            device_id=column(0, 1), device_id_type=MESH,
        )
        c.start()
        sends.append(c)

    def sib_forward(dz):
        sib(lbuf.at[pl.ds(LD * lplace(dz, 0), LD)], dz)

    def sib_wait(dz):
        ref = lbuf.at[pl.ds(LD * lplace(dz, 1), LD)]
        pltpu.make_async_copy(ref, ref, sr_sem.at[dz]).wait()

    def qrows(a, b, half):
        return qbuf.at[pl.ds(QD * qslot(a, b) + 16 * half, 16)]

    def q_copy(src, dst, n, to):
        c = pltpu.make_async_remote_copy(
            src_ref=src, dst_ref=dst, send_sem=qs_sem.at[n],
            recv_sem=qr_sem.at[n], device_id=plane(to[0] % 4, to[1] % 4),
            device_id_type=MESH,
        )
        c.start()
        sends.append(c)

    def q_own(a, b, to):
        for half in range(2):
            dst = qbuf.at[pl.ds(QD * qslot(a, b) + 16 * half, 16), pl.ds(0, BINS)]
            q_copy(q_in.at[pl.ds(16 * half, 16)], dst, qslot(a, b) * 2 + half, to)

    EXT = ((1, 0), (3, 0), (0, 1), (0, 3))

    def ext_ref(a, b):
        return qbuf.at[pl.ds(QD * qslot(a, b), QD), pl.ds(BINS, 128)]

    def q_ext(a, b, to):
        q_copy(ext_ref(0, 0), ext_ref(a, b), 32 + EXT.index((a, b)), to)

    def ext_wait(a, b):
        ref = ext_ref(a, b)
        pltpu.make_async_copy(ref, ref, qr_sem.at[32 + EXT.index((a, b))]).wait()

    def q_send(a, b, half, to):
        na, nb = a - to[0], b - to[1]
        q_copy(qrows(a, b, half), qrows(na, nb, half), qslot(na, nb) * 2 + half, to)

    def q_wait(a, b, half):
        rows = pl.ds(QD * qslot(a, b) + 16 * half, 16)
        ref = qbuf.at[rows, pl.ds(0, BINS)] if (a, b) in EXT else qbuf.at[rows]
        pltpu.make_async_copy(ref, ref, qr_sem.at[qslot(a, b) * 2 + half]).wait()

    for n in range(3):
        l_send(l_in.at[pl.ds(CH * n, CH)], 7, n, 1)
        l_send(l_in.at[pl.ds(CH * (2 - n), CH)], 1, 2 - n, 7)
    sib(l_in, 0)
    q_own(3, 0, (1, 0))
    q_own(1, 0, (3, 0))

    lane = lax.broadcasted_iota(jnp.int32, (1, 128), 1)

    def squares(ref, rows):
        acc = jnp.zeros((rows, 128), jnp.float32)
        for t in range(BINS // 128):
            v = ref[0:rows, 128 * t:128 * (t + 1)].astype(jnp.float32)
            acc = acc + v * v
        return acc

    for c in small:
        c.wait()
    loc_q.wait()
    total = jnp.sum(squares(qbuf, QD), axis=1, keepdims=True)
    qscale = lax.rsqrt(total * (1.0 / BINS) + EPS) * (1.0 / math.sqrt(BINS))
    high = qscale.astype(jnp.bfloat16).astype(jnp.float32)
    mid = (qscale - high).astype(jnp.bfloat16).astype(jnp.float32)
    rest = qscale - high - mid
    row = lax.broadcasted_iota(jnp.int32, (QD, 128), 0)
    col = lax.broadcasted_iota(jnp.int32, (QD, 128), 1)
    ext = jnp.where(row < QBLK, w_in[0], w_in[1]).astype(jnp.float32)
    for i, piece in enumerate((high, mid, rest)):
        ext = jnp.where(col == i + 1, piece, ext)
    qbuf[0:QD, BINS:WIDE] = ext.astype(jnp.bfloat16)
    q_ext(3, 0, (1, 0))
    q_ext(1, 0, (3, 0))
    q_ext(0, 3, (0, 1))
    q_ext(0, 1, (0, 3))

    loc_l.wait()
    acc = squares(lbuf, LD)
    acc = jnp.concatenate([acc, jnp.zeros((128 - LD, 128), jnp.float32)], axis=0)
    total = jnp.sum(acc.T, axis=0, keepdims=True)
    lscale = lax.rsqrt(total * (1.0 / BINS) + EPS)
    row_band = jnp.zeros((1, 128), jnp.int32)
    for j in range(LD // LBLK):
        row_band = jnp.where(lane >= 64 + LBLK * j, b_in[j], row_band)
    lmeta[0] = jnp.where(lane < 64, lscale, row_band.astype(jnp.float32))
    m_send(0, 7, 1)
    m_send(0, 1, 7)
    q_own(0, 3, (0, 1))
    q_own(0, 1, (0, 3))

    qt32[:, 0:MAXSHIFT, :] = jnp.zeros((4, MAXSHIFT, 128), jnp.float32)
    qt32[:, BINS + MAXSHIFT:PAD, :] = jnp.zeros((4, MAXSHIFT, 128), jnp.float32)
    best[...] = jnp.full(best.shape, -jnp.inf, jnp.float32)

    eye_r = lax.broadcasted_iota(jnp.int32, (256, 256), 0)
    eye_c = lax.broadcasted_iota(jnp.int32, (256, 256), 1)
    eye = (eye_r == eye_c).astype(jnp.float32).astype(jnp.bfloat16)

    def turned(h, c0, width):
        return lax.dot_general(
            eye[0:width, 0:width], qbuf[256 * h:256 * h + 256, c0:c0 + width],
            (((1,), (1,)), ((), ())), preferred_element_type=jnp.float32,
        )

    def prepare(h):
        cols = slice(256 * h, 256 * h + 256)
        for c0 in range(0, BINS, 256):
            v = turned(h, c0, 256)
            r0 = MAXSHIFT + c0
            qt32[2 * h, r0:r0 + 256, :] = v[:, 0:128]
            qt32[2 * h + 1, r0:r0 + 256, :] = v[:, 128:256]
        ext = turned(h, BINS, 128)
        qrow[0:1, cols] = ext[1:2] + ext[2:3] + ext[3:4]
        qrow[1:2, cols] = ext[0:1]
        offs = [s_in[k] + MAXSHIFT for k in range(NOFF)]

        @pl.loop(0, BINS // 128)
        def _(i):
            r0 = pl.multiple_of(i * 128, 128)
            for k in range(NOFF):
                for t in (2 * h, 2 * h + 1):
                    v = qt32[t, pl.ds(r0 + offs[k], 128), :]
                    qtk[k, pl.ds(r0, 128), 128 * t:128 * t + 128] = v.astype(jnp.bfloat16)

    def multiply(row, rows, h):
        cols = slice(256 * h, 256 * h + 256)
        for k in range(NOFF):
            d = jnp.dot(
                lbuf[row:row + rows, :], qtk[k, :, cols], preferred_element_type=jnp.float32
            )
            if k:
                d = jnp.maximum(sc[row:row + rows, cols], d)
            sc[row:row + rows, cols] = d

    def select(g0, g1, tiles):
        @pl.loop(g0, g1)
        def _(g):
            for t in tiles:
                cols = slice(128 * t, 128 * t + 128)
                scale_q = jnp.broadcast_to(qrow[0:1, cols], (8, 128))
                low = jnp.broadcast_to(qrow[1:2, cols], (8, 128))
                high = low + float(SPAN)
                vals = []
                for i in range(16):
                    r = pl.multiple_of(g * 128 + 8 * i, 8)
                    band = lband[pl.ds(r, 8), :]
                    v = sc[pl.ds(r, 8), cols] * scale_q * lsc[pl.ds(r, 8), :]
                    keep = (band >= low) & (band < high)
                    vals.append(jnp.where(keep, v, MASKED))
                vals = sort16(vals)
                vals = merge16([best[t, i] for i in range(16)], vals)
                for i in range(16):
                    best[t, i] = vals[i]

    def q_first(a, half):
        if half == (1 if a == 1 else 0):
            ext_wait(a, 0)
        q_wait(a, 0, half)
        if (a, half) == (1, 1):
            q_send(1, 0, 1, (-1, 0))
        if (a, half) == (3, 0):
            q_send(3, 0, 0, (1, 0))
        q_send(a, 0, half, (0, 1))
        q_send(a, 0, half, (0, -1))

    def q_across(half):
        q_wait(2, 0, half)
        q_send(2, 0, half, (0, 1))
        q_send(2, 0, half, (0, -1))

    def q_second(a, half):
        b = 1 if half else 3
        if a == 0:
            ext_wait(0, b)
        q_wait(a, b, half)
        q_send(a, b, half, (0, -1) if half else (0, 1))

    def q_rest(a):
        q_wait(a, 1, 0)
        q_wait(a, 3, 1)

    q_first(3, 0)
    q_first(1, 1)
    l_forward(1, 0)
    l_forward(1, 1)
    q_first(1, 0)
    q_first(3, 1)
    m_forward(1)
    l_forward(1, 2)
    q_across(0)
    q_second(0, 0)
    q_across(1)
    q_second(3, 0)
    sib_forward(1)
    sib_forward(7)
    q_second(1, 1)
    l_forward(2, 0)
    q_second(0, 1)
    q_rest(0)
    q_rest(1)
    q_second(1, 0)
    prepare(0)
    m_forward(2)
    l_forward(2, 1)
    q_second(2, 0)
    q_second(3, 1)
    l_forward(2, 2)
    sib_forward(2)
    sib_forward(6)
    q_second(2, 1)
    for dz in (0, 1, 7):
        sib_wait(dz)
    multiply(0, 288, 0)
    sib_wait(2)
    sib_wait(6)
    multiply(288, 192, 0)
    l_forward(3, 0)
    l_wait(5, 1)
    l_wait(3, 1)
    l_middle()
    m_forward(3)
    q_rest(3)
    q_rest(2)
    for a in range(4):
        q_wait(a, 2, 0)
        q_wait(a, 2, 1)
    prepare(1)
    l_wait(5, 2)
    l_wait(3, 0)
    sib_forward(3)
    sib_forward(5)
    multiply(0, 288, 1)
    m_wait(4)
    pltpu.make_async_remote_copy(
        src_ref=lmeta.at[pl.ds(0, 8)], dst_ref=lmeta.at[pl.ds(8, 8)], send_sem=ms_sem.at[0],
        recv_sem=mr_sem.at[0], device_id=column(0, 1), device_id_type=MESH,
    ).start()
    multiply(288, 192, 1)

    pltpu.make_async_copy(lmeta.at[pl.ds(8, 8)], lmeta.at[pl.ds(8, 8)], mr_sem.at[0]).wait()
    for c in range(2):
        for dz in range(8):
            m = jnp.broadcast_to(lmeta[8 * c + dz], (128, 128)).T
            r = LD * lplace(dz, c)
            lsc[r:r + LD, :] = m[0:LD]
            lband[r:r + LD, :] = m[64:64 + LD]
    for n in range(3):
        l_wait(4, n)
    sib_forward(4)
    sib_wait(3)
    sib_wait(5)
    multiply(480, 192, 1)
    select(0, 5, (2, 3))
    sib_wait(4)

    def finish(t):
        vals = [best[t, i] for i in range(16)]
        for sh in (4, 2, 1):
            vals = merge16(vals, [pltpu.roll(v, sh, 0) for v in vals])
        for i in range(16):
            fin[t, i:i + 1, :] = vals[i][0:1]
        for p in (3, 2, 1, 0):
            n = 4 * t + p
            if n == 0:
                continue
            a, b = SLOTS[n]
            pltpu.make_async_remote_copy(
                src_ref=fin.at[t], dst_ref=got.at[n], send_sem=f_sem.at[0],
                recv_sem=f_sem.at[1], device_id=plane(a, b), device_id_type=MESH,
            ).start()

    for h in (1, 0):
        if h == 0:
            multiply(480, 192, 0)
            select(0, 5, (0, 1))
        multiply(672, 96, h)
        for t in (2 * h + 1, 2 * h):
            select(5, 6, (t,))
            finish(t)
    got[0] = fin[0]
    for c in sends:
        c.wait_send()
    pltpu.make_async_copy(lmeta.at[pl.ds(0, 8)], lmeta.at[pl.ds(0, 8)], ms_sem.at[0]).wait()
    pltpu.make_async_copy(got.at[pl.ds(1, 15)], got.at[pl.ds(1, 15)], f_sem.at[0]).wait()
    pltpu.make_async_copy(got.at[pl.ds(1, 15)], got.at[pl.ds(1, 15)], f_sem.at[1]).wait()

    part = lax.div(lax.broadcasted_iota(jnp.int32, (8, 128), 1), QD)
    vals = []
    for r in range(16):
        rows = []
        for t in range(4):
            v = got[4 * t, r:r + 1, :]
            for p in range(1, 4):
                v = jnp.where(part[0:1] == p, got[4 * t + p, r:r + 1, :], v)
            rows.append(v)
        vals.append(jnp.concatenate(rows + rows, axis=0))
    for sh in (2, 1):
        vals = merge16(vals, [pltpu.roll(v, sh, 0) for v in vals])
    for sh in (64, 32):
        vals = merge16(vals, [pltpu.roll(v, sh, 1) for v in vals])
    for i in range(TOPK):
        out[i:i + 1, :] = vals[i][0:1, 0:QD]


def local(queries, windows, library, bands, shifts):
    dma = pltpu.SemaphoreType.DMA
    f32, bf16 = jnp.float32, jnp.bfloat16
    hbm = pl.BlockSpec(memory_space=pltpu.HBM)
    return pl.pallas_call(
        kernel,
        out_shape=jax.ShapeDtypeStruct((TOPK, QD), f32),
        in_specs=[hbm] * 5,
        out_specs=pl.BlockSpec(memory_space=pltpu.VMEM),
        scratch_shapes=[
            pltpu.SMEM((2,), jnp.int32),
            pltpu.SMEM((6,), jnp.int32),
            pltpu.SMEM((NOFF,), jnp.int32),
            pltpu.VMEM((NQ, WIDE), bf16),
            pltpu.VMEM((NL, BINS), bf16),
            pltpu.VMEM((4, PAD, 128), f32),
            pltpu.VMEM((NOFF, BINS, NQ), bf16),
            pltpu.VMEM((NL, NQ), f32),
            pltpu.VMEM((NL, 128), f32),
            pltpu.VMEM((NL, 128), f32),
            pltpu.VMEM((8, NQ), f32),
            pltpu.VMEM((4, 16, 8, 128), f32),
            pltpu.VMEM((16, 1, 128), f32),
            pltpu.VMEM((4, 16, 128), f32),
            pltpu.VMEM((16, 16, 128), f32),
            dma((5,)), dma((36,)), dma((36,)), dma((21,)), dma((21,)),
            dma((8,)), dma((8,)), dma((8,)), dma((8,)), dma((2,)),
        ],
        compiler_params=pltpu.CompilerParams(
            collective_id=0, has_side_effects=True, vmem_limit_bytes=62 * 2**20
        ),
        cost_estimate=pl.CostEstimate(
            flops=2 * NQ * NL * BINS * NOFF, bytes_accessed=2 * (QD + LD) * BINS, transcendentals=0
        ),
    )(queries, windows, library, bands, shifts).T


def solution(mesh):
    return jax.shard_map(
        local,
        mesh=mesh,
        in_specs=(
            P(("blk", "grp"), None),
            P(("blk", "grp")),
            P(("blk", "grp"), None),
            P(("blk", "grp")),
            P(),
        ),
        out_specs=P(("blk", "grp"), None),
        check_vma=False,
    )
```

```python
import functools
import math

import jax
import jax.numpy as jnp
from jax import lax
from jax.experimental import pallas as pl
from jax.experimental.pallas import tpu as pltpu
from jax.sharding import PartitionSpec as P

BINS = 2048
NOFF = 4
TOPK = 16
MAXSHIFT = 24
QBLK = 16
LBLK = 8
SPAN = 4
EPS = 1e-06
MASKED = -8.0

QD = 32
LD = 48
CH = 16
NQ = 16 * QD
NL = 16 * LD
PAD = BINS + 2 * MAXSHIFT
WIDE = BINS + 128
MESH = pl.DeviceIdType.MESH

SLOTS = [
    (0, 0), (1, 0), (3, 0), (2, 0),
    (0, 1), (0, 3), (1, 1), (1, 3),
    (3, 1), (3, 3), (2, 1), (2, 3),
    (0, 2), (1, 2), (3, 2), (2, 2),
]


def qslot(a, b):
    return SLOTS.index((a % 4, b % 4))


def lplace(dz, c):
    dz %= 8
    if dz == 0:
        return c
    if dz == 4:
        return 14 + c
    d = min(dz, 8 - dz)
    return 2 + 4 * (d - 1) + 2 * c + (1 if dz > 4 else 0)


def batcher(n):
    pairs = []
    p = 1
    while p < n:
        k = p
        while k >= 1:
            for j in range(k % p, n - k, 2 * k):
                for i in range(min(k, n - j - k)):
                    if (i + j) // (2 * p) == (i + j + k) // (2 * p):
                        pairs.append((i + j, i + j + k))
            k //= 2
        p *= 2
    return pairs


SORT16 = batcher(16)


def sort16(v):
    v = list(v)
    for i, j in SORT16:
        v[i], v[j] = jnp.maximum(v[i], v[j]), jnp.minimum(v[i], v[j])
    return v


def merge16(a, b):
    v = [jnp.maximum(a[i], b[15 - i]) for i in range(16)]
    for d in (8, 4, 2, 1):
        for i in range(16):
            if not i & d:
                v[i], v[i + d] = jnp.maximum(v[i], v[i + d]), jnp.minimum(v[i], v[i + d])
    return v


def kernel(
    q_in, w_hbm, l_in, b_hbm, s_hbm, out,
    w_in, b_in, s_in, qbuf, lbuf, qt32, qtk, sc, lsc, lband, qrow, best, lmeta, fin, got,
    loc_sem, qs_sem, qr_sem, ls_sem, lr_sem, ss_sem, sr_sem, ms_sem, mr_sem, f_sem,
):
    blk = lax.axis_index("blk")
    grp = lax.axis_index("grp")
    core = lax.rem(blk, 2)
    z = lax.rem(lax.div(blk, 2), 8)
    x = lax.div(grp, 2)
    y = lax.rem(grp, 2) * 2 + lax.div(blk, 16)

    def place(px, py, pz, pc):
        return {
            "blk": (lax.rem(py, 2) * 8 + pz) * 2 + pc,
            "grp": px * 2 + lax.div(py, 2),
        }

    def plane(a, b):
        dx = a * (1 - core) + b * core
        dy = b * (1 - core) + a * core
        return place(lax.rem(x + dx, 4), lax.rem(y + dy, 4), z, core)

    def column(dz, dc):
        return place(x, y, lax.rem(z + dz, 8), core + dc * (1 - 2 * core))

    barrier = pltpu.get_barrier_semaphore()
    near = [plane(1, 0), plane(3, 0), plane(0, 1), plane(0, 3)]
    near += [column(1, 0), column(7, 0), column(0, 1)]
    for peer in near:
        pl.semaphore_signal(barrier, inc=1, device_id=peer, device_id_type=MESH)
    loc_q = pltpu.make_async_copy(q_in, qbuf.at[pl.ds(0, QD), pl.ds(0, BINS)], loc_sem.at[0])
    loc_l = pltpu.make_async_copy(l_in, lbuf.at[pl.ds(0, LD)], loc_sem.at[1])
    loc_q.start()
    loc_l.start()
    small = [
        pltpu.make_async_copy(src, dst, loc_sem.at[2 + i])
        for i, (src, dst) in enumerate(((w_hbm, w_in), (b_hbm, b_in), (s_hbm, s_in)))
    ]
    for c in small:
        c.start()
    pl.semaphore_wait(barrier, len(near))

    sends = []

    UP = ((0, 32), (32, 16))
    DOWN = ((16, 32), (0, 16))

    def lrows(dz, part):
        if dz == 4:
            return lbuf.at[pl.ds(LD * lplace(4, 0), LD)]
        r, n = (UP if dz > 4 else DOWN)[part]
        return lbuf.at[pl.ds(LD * lplace(dz, 0) + r, n)]

    def l_copy(src, dst, n_send, n_recv, step):
        c = pltpu.make_async_remote_copy(
            src_ref=src, dst_ref=dst, send_sem=ls_sem.at[n_send],
            recv_sem=lr_sem.at[n_recv], device_id=column(step, 0), device_id_type=MESH,
        )
        c.start()
        sends.append(c)

    def l_send(src, dz, part, step):
        n = 2 * dz + part
        l_copy(src, lrows(dz, part), n, n, step)

    def l_wait(dz, part):
        ref = lrows(dz, part)
        pltpu.make_async_copy(ref, ref, lr_sem.at[2 * dz + part]).wait()

    def l_forward(d, part):
        l_wait(8 - d, part)
        l_wait(d, part)
        l_send(lrows(8 - d, part), 7 - d, part, 1)
        l_send(lrows(d, part), d + 1, part, 7)

    def l_last():
        l_wait(5, 0)
        l_wait(3, 0)
        up, down, far = (LD * lplace(dz, 0) for dz in (5, 3, 4))
        mid = up * (1 - core) + down * core + CH
        for i, (src, r, step) in enumerate(
            ((up, 0, 1), (down + 2 * CH, 2 * CH, 7), (mid, CH, 1 + 6 * core))
        ):
            src = lbuf.at[pl.ds(pl.multiple_of(src, CH), CH)]
            l_copy(src, lbuf.at[pl.ds(far + r, CH)], (8, 9, 0)[i], 8, step)

    def m_send(src_dz, dst_dz, step):
        c = pltpu.make_async_remote_copy(
            src_ref=lmeta.at[src_dz], dst_ref=lmeta.at[dst_dz],
            send_sem=ms_sem.at[dst_dz], recv_sem=mr_sem.at[dst_dz],
            device_id=column(step, 0), device_id_type=MESH,
        )
        c.start()
        sends.append(c)

    def m_wait(dz):
        pltpu.make_async_copy(lmeta.at[dz], lmeta.at[dz], mr_sem.at[dz]).wait()

    def m_forward(d):
        m_wait(8 - d)
        m_wait(d)
        m_send(8 - d, 7 - d, 1)
        if d < 3:
            m_send(d, d + 1, 7)

    def sib(src, d):
        rows = src.shape[0]
        c = pltpu.make_async_remote_copy(
            src_ref=src, dst_ref=lbuf.at[pl.ds(LD * lplace(d, 1), rows)],
            send_sem=ss_sem.at[d], recv_sem=sr_sem.at[d],
            device_id=column(0, 1), device_id_type=MESH,
        )
        c.start()
        sends.append(c)

    def sib_forward(d):
        sib(lbuf.at[pl.ds(LD * lplace(d, 0), LD if d == 4 else 2 * LD)], d)

    def sib_wait(d):
        ref = lbuf.at[pl.ds(LD * lplace(d, 1), 2 * LD if d in (1, 2, 3) else LD)]
        pltpu.make_async_copy(ref, ref, sr_sem.at[d]).wait()

    def qrows(a, b, half):
        return qbuf.at[pl.ds(QD * qslot(a, b) + 16 * half, 16)]

    def is_last(a, b, half):
        return b == 2 or (a, b, half) in ((3, 1, 0), (3, 3, 1), (2, 1, 0), (2, 3, 1))

    def q_copy(src, dst, n, to, last=False):
        c = pltpu.make_async_remote_copy(
            src_ref=src, dst_ref=dst, send_sem=qs_sem.at[n],
            recv_sem=qr_sem.at[36 if last else n], device_id=plane(to[0] % 4, to[1] % 4),
            device_id_type=MESH,
        )
        c.start()
        sends.append(c)

    def q_own(a, b, to):
        for half in range(2):
            dst = qbuf.at[pl.ds(QD * qslot(a, b) + 16 * half, 16), pl.ds(0, BINS)]
            q_copy(q_in.at[pl.ds(16 * half, 16)], dst, qslot(a, b) * 2 + half, to)

    EXT = ((1, 0), (3, 0), (0, 1), (0, 3))

    def ext_ref(a, b):
        return qbuf.at[pl.ds(QD * qslot(a, b), QD), pl.ds(BINS, 128)]

    def q_ext(a, b, to):
        q_copy(ext_ref(0, 0), ext_ref(a, b), 32 + EXT.index((a, b)), to)

    def ext_wait(a, b):
        ref = ext_ref(a, b)
        pltpu.make_async_copy(ref, ref, qr_sem.at[32 + EXT.index((a, b))]).wait()

    def q_send(a, b, half, to):
        na, nb = (a - to[0]) % 4, (b - to[1]) % 4
        n = qslot(na, nb) * 2 + half
        q_copy(qrows(a, b, half), qrows(na, nb, half), n, to, is_last(na, nb, half))

    def q_wait(a, b, half):
        rows = pl.ds(QD * qslot(a, b) + 16 * half, 16)
        ref = qbuf.at[rows, pl.ds(0, BINS)] if (a, b) in EXT else qbuf.at[rows]
        pltpu.make_async_copy(ref, ref, qr_sem.at[qslot(a, b) * 2 + half]).wait()

    for part in range(2):
        l_send(l_in.at[pl.ds(*UP[part])], 7, part, 1)
        l_send(l_in.at[pl.ds(*DOWN[part])], 1, part, 7)
    sib(l_in, 0)
    q_own(3, 0, (1, 0))
    q_own(1, 0, (3, 0))

    lane = lax.broadcasted_iota(jnp.int32, (1, 128), 1)

    def squares(ref, rows):
        acc = jnp.zeros((rows, 128), jnp.float32)
        for t in range(BINS // 128):
            v = ref[0:rows, 128 * t:128 * (t + 1)].astype(jnp.float32)
            acc = acc + v * v
        return acc

    for c in small:
        c.wait()
    loc_q.wait()
    total = jnp.sum(squares(qbuf, QD), axis=1, keepdims=True)
    qscale = lax.rsqrt(total * (1.0 / BINS) + EPS) * (1.0 / math.sqrt(BINS))
    high = qscale.astype(jnp.bfloat16).astype(jnp.float32)
    mid = (qscale - high).astype(jnp.bfloat16).astype(jnp.float32)
    rest = qscale - high - mid
    row = lax.broadcasted_iota(jnp.int32, (QD, 128), 0)
    col = lax.broadcasted_iota(jnp.int32, (QD, 128), 1)
    ext = jnp.where(row < QBLK, w_in[0], w_in[1]).astype(jnp.float32)
    for i, piece in enumerate((high, mid, rest)):
        ext = jnp.where(col == i + 1, piece, ext)
    qbuf[0:QD, BINS:WIDE] = ext.astype(jnp.bfloat16)
    q_ext(3, 0, (1, 0))
    q_ext(1, 0, (3, 0))
    q_ext(0, 3, (0, 1))
    q_ext(0, 1, (0, 3))

    loc_l.wait()
    acc = squares(lbuf, LD)
    acc = jnp.concatenate([acc, jnp.zeros((128 - LD, 128), jnp.float32)], axis=0)
    total = jnp.sum(acc.T, axis=0, keepdims=True)
    lscale = lax.rsqrt(total * (1.0 / BINS) + EPS)
    row_band = jnp.zeros((1, 128), jnp.int32)
    for j in range(LD // LBLK):
        row_band = jnp.where(lane >= 64 + LBLK * j, b_in[j], row_band)
    lmeta[0] = jnp.where(lane < 64, lscale, row_band.astype(jnp.float32))
    m_send(0, 7, 1)
    m_send(0, 1, 7)
    q_own(0, 3, (0, 1))
    q_own(0, 1, (0, 3))

    qt32[:, 0:MAXSHIFT, :] = jnp.zeros((4, MAXSHIFT, 128), jnp.float32)
    qt32[:, BINS + MAXSHIFT:PAD, :] = jnp.zeros((4, MAXSHIFT, 128), jnp.float32)

    eye_r = lax.broadcasted_iota(jnp.int32, (256, 256), 0)
    eye_c = lax.broadcasted_iota(jnp.int32, (256, 256), 1)
    eye = (eye_r == eye_c).astype(jnp.float32).astype(jnp.bfloat16)

    def turned(h, c0, width):
        return lax.dot_general(
            eye[0:width, 0:width], qbuf[256 * h:256 * h + 256, c0:c0 + width],
            (((1,), (1,)), ((), ())), preferred_element_type=jnp.float32,
        )

    def prepare(h):
        cols = slice(256 * h, 256 * h + 256)
        for c0 in range(0, BINS, 256):
            v = turned(h, c0, 256)
            r0 = MAXSHIFT + c0
            qt32[2 * h, r0:r0 + 256, :] = v[:, 0:128]
            qt32[2 * h + 1, r0:r0 + 256, :] = v[:, 128:256]
        ext = turned(h, BINS, 128)
        qrow[0:1, cols] = ext[1:2] + ext[2:3] + ext[3:4]
        qrow[1:2, cols] = ext[0:1]
        offs = [s_in[k] + MAXSHIFT for k in range(NOFF)]

        @pl.loop(0, BINS // 128)
        def _(i):
            r0 = pl.multiple_of(i * 128, 128)
            for k in range(NOFF):
                for t in (2 * h, 2 * h + 1):
                    v = qt32[t, pl.ds(r0 + offs[k], 128), :]
                    qtk[k, pl.ds(r0, 128), 128 * t:128 * t + 128] = v.astype(jnp.bfloat16)

    def multiply(row, rows, h, beside=()):
        beside = list(beside)
        each = -(-len(beside) // NOFF)
        cols = slice(256 * h, 256 * h + 256)
        for k in range(NOFF):
            d = jnp.dot(
                lbuf[row:row + rows, :], qtk[k, :, cols], preferred_element_type=jnp.float32
            )
            if k:
                d = jnp.maximum(sc[row:row + rows, cols], d)
            sc[row:row + rows, cols] = d
            for f in beside[each * k:each * (k + 1)]:
                f()

    def select(g, t):
        cols = slice(128 * t, 128 * t + 128)
        scale_q = jnp.broadcast_to(qrow[0:1, cols], (8, 128))
        low = jnp.broadcast_to(qrow[1:2, cols], (8, 128))
        high = low + float(SPAN)
        vals = []
        for i in range(16):
            r = g * 128 + 8 * i
            band = lband[r:r + 8, :]
            v = sc[r:r + 8, cols] * scale_q * lsc[r:r + 8, :]
            keep = (band >= low) & (band < high)
            vals.append(jnp.where(keep, v, MASKED))
        vals = sort16(vals)
        if g:
            vals = merge16([best[t, i] for i in range(16)], vals)
        for i in range(16):
            best[t, i] = vals[i]

    def selects(groups, tiles):
        return [functools.partial(select, g, t) for g in groups for t in tiles]

    def spread(c, dz):
        m = jnp.broadcast_to(lmeta[8 * c + dz], (128, 128)).T
        r = LD * lplace(dz, c)
        lsc[r:r + LD, :] = m[0:LD]
        lband[r:r + LD, :] = m[64:64 + LD]

    def q_first(a, half):
        if half == 0:
            ext_wait(a, 0)
        q_wait(a, 0, half)
        if (a, half) == (1, 1):
            q_send(1, 0, 1, (-1, 0))
        if (a, half) == (3, 0):
            q_send(3, 0, 0, (1, 0))
        q_send(a, 0, half, (0, 1))
        q_send(a, 0, half, (0, -1))

    def q_across(half):
        q_wait(2, 0, half)
        q_send(2, 0, half, (0, 1))
        q_send(2, 0, half, (0, -1))

    def q_second(a, half):
        b = 1 if half else 3
        if a == 0:
            ext_wait(0, b)
        q_wait(a, b, half)
        q_send(a, b, half, (0, -1) if half else (0, 1))

    def q_rest(a):
        q_wait(a, 1, 0)
        q_wait(a, 3, 1)

    q_first(1, 0)
    q_first(3, 0)
    l_forward(1, 0)
    q_first(1, 1)
    m_forward(1)
    l_forward(1, 1)
    q_second(0, 1)
    q_first(3, 1)
    q_across(0)
    sib_forward(1)
    q_second(3, 0)
    q_second(0, 0)
    q_second(1, 0)
    q_across(1)
    q_second(1, 1)
    m_forward(2)
    l_forward(2, 0)
    q_rest(0)
    q_rest(1)
    prepare(0)
    q_second(3, 1)
    l_forward(2, 1)
    q_second(2, 0)
    sib_forward(2)
    m_forward(3)
    q_second(2, 1)
    sib_wait(0)
    sib_wait(1)
    multiply(0, 288, 0)
    sib_wait(2)
    multiply(288, 192, 0)
    l_last()
    ref = qbuf.at[pl.ds(0, 192)]
    pltpu.make_async_copy(ref, ref, qr_sem.at[36]).wait()
    prepare(1)
    m_wait(4)
    pltpu.make_async_remote_copy(
        src_ref=lmeta.at[pl.ds(0, 8)], dst_ref=lmeta.at[pl.ds(8, 8)], send_sem=ms_sem.at[0],
        recv_sem=mr_sem.at[0], device_id=column(0, 1), device_id_type=MESH,
    ).start()
    multiply(0, 288, 1, [functools.partial(spread, 0, dz) for dz in range(8)])
    l_wait(5, 1)
    l_wait(3, 1)
    sib_forward(3)
    pltpu.make_async_copy(lmeta.at[pl.ds(8, 8)], lmeta.at[pl.ds(8, 8)], mr_sem.at[0]).wait()
    multiply(288, 192, 1, [functools.partial(spread, 1, dz) for dz in range(8)])
    l_wait(4, 0)
    sib_forward(4)
    sib_wait(3)
    multiply(480, 192, 1, selects(range(3), (2, 3)))
    sib_wait(4)

    def finish(t):
        vals = [best[t, i] for i in range(16)]
        for sh in (4, 2, 1):
            vals = merge16(vals, [pltpu.roll(v, sh, 0) for v in vals])
        for i in range(16):
            fin[t, i:i + 1, :] = vals[i][0:1]
        for p in (3, 2, 1, 0):
            n = 4 * t + p
            if n == 0:
                continue
            a, b = SLOTS[n]
            pltpu.make_async_remote_copy(
                src_ref=fin.at[t], dst_ref=got.at[n], send_sem=f_sem.at[0],
                recv_sem=f_sem.at[1], device_id=plane(a, b), device_id_type=MESH,
            ).start()

    multiply(672, 96, 1, selects(range(3, 5), (2, 3)))
    for t in (3, 2):
        select(5, t)
        finish(t)
    multiply(480, 288, 0, selects(range(3), (0, 1)))
    for t in (1, 0):
        for g in range(3, 6):
            select(g, t)
        finish(t)
    got[0] = fin[0]
    for c in sends:
        c.wait_send()
    pltpu.make_async_copy(lmeta.at[pl.ds(0, 8)], lmeta.at[pl.ds(0, 8)], ms_sem.at[0]).wait()
    pltpu.make_async_copy(got.at[pl.ds(1, 15)], got.at[pl.ds(1, 15)], f_sem.at[0]).wait()
    pltpu.make_async_copy(got.at[pl.ds(1, 15)], got.at[pl.ds(1, 15)], f_sem.at[1]).wait()

    part = lax.div(lax.broadcasted_iota(jnp.int32, (8, 128), 1), QD)
    vals = []
    for r in range(16):
        rows = []
        for t in range(4):
            v = got[4 * t, r:r + 1, :]
            for p in range(1, 4):
                v = jnp.where(part[0:1] == p, got[4 * t + p, r:r + 1, :], v)
            rows.append(v)
        vals.append(jnp.concatenate(rows + rows, axis=0))
    for sh in (2, 1):
        vals = merge16(vals, [pltpu.roll(v, sh, 0) for v in vals])
    for sh in (64, 32):
        vals = merge16(vals, [pltpu.roll(v, sh, 1) for v in vals])
    for i in range(TOPK):
        out[i:i + 1, :] = vals[i][0:1, 0:QD]


def local(queries, windows, library, bands, shifts):
    dma = pltpu.SemaphoreType.DMA
    f32, bf16 = jnp.float32, jnp.bfloat16
    hbm = pl.BlockSpec(memory_space=pltpu.HBM)
    return pl.pallas_call(
        kernel,
        out_shape=jax.ShapeDtypeStruct((TOPK, QD), f32),
        in_specs=[hbm] * 5,
        out_specs=pl.BlockSpec(memory_space=pltpu.VMEM),
        scratch_shapes=[
            pltpu.SMEM((2,), jnp.int32),
            pltpu.SMEM((6,), jnp.int32),
            pltpu.SMEM((NOFF,), jnp.int32),
            pltpu.VMEM((NQ, WIDE), bf16),
            pltpu.VMEM((NL, BINS), bf16),
            pltpu.VMEM((4, PAD, 128), f32),
            pltpu.VMEM((NOFF, BINS, NQ), bf16),
            pltpu.VMEM((NL, NQ), f32),
            pltpu.VMEM((NL, 128), f32),
            pltpu.VMEM((NL, 128), f32),
            pltpu.VMEM((8, NQ), f32),
            pltpu.VMEM((4, 16, 8, 128), f32),
            pltpu.VMEM((16, 1, 128), f32),
            pltpu.VMEM((4, 16, 128), f32),
            pltpu.VMEM((16, 16, 128), f32),
            dma((5,)), dma((36,)), dma((37,)), dma((16,)), dma((16,)),
            dma((5,)), dma((5,)), dma((8,)), dma((8,)), dma((2,)),
        ],
        compiler_params=pltpu.CompilerParams(
            collective_id=0, has_side_effects=True, vmem_limit_bytes=62 * 2**20
        ),
        cost_estimate=pl.CostEstimate(
            flops=2 * NQ * NL * BINS * NOFF, bytes_accessed=2 * (QD + LD) * BINS, transcendentals=0
        ),
    )(queries, windows, library, bands, shifts).T


def solution(mesh):
    return jax.shard_map(
        local,
        mesh=mesh,
        in_specs=(
            P(("blk", "grp"), None),
            P(("blk", "grp")),
            P(("blk", "grp"), None),
            P(("blk", "grp")),
            P(),
        ),
        out_specs=P(("blk", "grp"), None),
        check_vma=False,
    )
```

```python
import functools
import math

import jax
import jax.numpy as jnp
from jax import lax
from jax.experimental import pallas as pl
from jax.experimental.pallas import tpu as pltpu
from jax.sharding import PartitionSpec as P

BINS = 2048
NOFF = 4
TOPK = 16
MAXSHIFT = 24
QBLK = 16
LBLK = 8
SPAN = 4
EPS = 1e-06
MASKED = -8.0

QD = 32
LD = 48
CH = 16
NQ = 16 * QD
NL = 16 * LD
PAD = BINS + 2 * MAXSHIFT
WIDE = BINS + 128
MESH = pl.DeviceIdType.MESH

SLOTS = [
    (0, 0), (1, 0), (3, 0), (2, 0),
    (0, 1), (0, 3), (1, 1), (1, 3),
    (3, 1), (3, 3), (2, 1), (2, 3),
    (0, 2), (1, 2), (3, 2), (2, 2),
]


def qslot(a, b):
    return SLOTS.index((a % 4, b % 4))


def lplace(dz, c):
    dz %= 8
    if dz == 0:
        return c
    if dz == 4:
        return 14 + c
    d = min(dz, 8 - dz)
    return 2 + 4 * (d - 1) + 2 * c + (1 if dz > 4 else 0)


def batcher(n):
    pairs = []
    p = 1
    while p < n:
        k = p
        while k >= 1:
            for j in range(k % p, n - k, 2 * k):
                for i in range(min(k, n - j - k)):
                    if (i + j) // (2 * p) == (i + j + k) // (2 * p):
                        pairs.append((i + j, i + j + k))
            k //= 2
        p *= 2
    return pairs


SORT16 = batcher(16)


def sort16(v):
    v = list(v)
    for i, j in SORT16:
        v[i], v[j] = jnp.maximum(v[i], v[j]), jnp.minimum(v[i], v[j])
    return v


def merge16(a, b):
    v = [jnp.maximum(a[i], b[15 - i]) for i in range(16)]
    for d in (8, 4, 2, 1):
        for i in range(16):
            if not i & d:
                v[i], v[i + d] = jnp.maximum(v[i], v[i + d]), jnp.minimum(v[i], v[i + d])
    return v


def kernel(
    q_in, w_hbm, l_in, b_hbm, s_hbm, out,
    w_in, b_in, s_in, qbuf, lbuf, qt32, qtk, sc, lsc, lband, qrow, best, lmeta, fin, got,
    loc_sem, left_sem, qr_sem, lr_sem, sr_sem, mr_sem, f_sem,
):
    blk = lax.axis_index("blk")
    grp = lax.axis_index("grp")
    core = lax.rem(blk, 2)
    z = lax.rem(lax.div(blk, 2), 8)
    x = lax.div(grp, 2)
    y = lax.rem(grp, 2) * 2 + lax.div(blk, 16)

    def place(px, py, pz, pc):
        return {
            "blk": (lax.rem(py, 2) * 8 + pz) * 2 + pc,
            "grp": px * 2 + lax.div(py, 2),
        }

    def plane(a, b):
        dx = a * (1 - core) + b * core
        dy = b * (1 - core) + a * core
        return place(lax.rem(x + dx, 4), lax.rem(y + dy, 4), z, core)

    def column(dz, dc):
        return place(x, y, lax.rem(z + dz, 8), core + dc * (1 - 2 * core))

    barrier = pltpu.get_barrier_semaphore()
    near = [plane(1, 0), plane(3, 0), plane(0, 1), plane(0, 3)]
    near += [column(1, 0), column(7, 0), column(0, 1)]
    for peer in near:
        pl.semaphore_signal(barrier, inc=1, device_id=peer, device_id_type=MESH)
    loc_q = pltpu.make_async_copy(q_in, qbuf.at[pl.ds(0, QD), pl.ds(0, BINS)], loc_sem.at[0])
    loc_l = pltpu.make_async_copy(l_in, lbuf.at[pl.ds(0, LD)], loc_sem.at[1])
    loc_q.start()
    loc_l.start()
    small = [
        pltpu.make_async_copy(src, dst, loc_sem.at[2 + i])
        for i, (src, dst) in enumerate(((w_hbm, w_in), (b_hbm, b_in), (s_hbm, s_in)))
    ]
    for c in small:
        c.start()
    pl.semaphore_wait(barrier, len(near))

    def wait_all(ref, sem):
        pltpu.make_async_copy(ref, ref, sem).wait()

    UP = ((0, 32), (32, 16))
    DOWN = ((16, 32), (0, 16))

    def lrows(dz, part):
        if dz == 4:
            return lbuf.at[pl.ds(LD * lplace(4, 0), LD)]
        r, n = (UP if dz > 4 else DOWN)[part]
        return lbuf.at[pl.ds(LD * lplace(dz, 0) + r, n)]

    def l_copy(src, dst, n, step):
        c = pltpu.make_async_remote_copy(
            src_ref=src, dst_ref=dst, send_sem=left_sem.at[0],
            recv_sem=lr_sem.at[n], device_id=column(step, 0), device_id_type=MESH,
        )
        c.start()

    def l_send(src, dz, part, step):
        l_copy(src, lrows(dz, part), 2 * min(dz, 8 - dz) + part, step)

    def l_wait(d, part):
        wait_all(lbuf.at[pl.ds(0, LD if d == 4 else (64, 32)[part])], lr_sem.at[2 * d + part])

    def l_forward(d, part):
        l_wait(d, part)
        l_send(lrows(8 - d, part), 7 - d, part, 1)
        l_send(lrows(d, part), d + 1, part, 7)

    def l_last():
        l_wait(3, 0)
        up, down, far = (LD * lplace(dz, 0) for dz in (5, 3, 4))
        mid = up * (1 - core) + down * core + CH
        for src, r, step in (
            (up, 0, 1), (down + 2 * CH, 2 * CH, 7), (mid, CH, 1 + 6 * core)
        ):
            src = lbuf.at[pl.ds(pl.multiple_of(src, CH), CH)]
            l_copy(src, lbuf.at[pl.ds(far + r, CH)], 8, step)

    def m_send(src_dz, dst_dz, step):
        c = pltpu.make_async_remote_copy(
            src_ref=lmeta.at[src_dz], dst_ref=lmeta.at[dst_dz],
            send_sem=left_sem.at[1], recv_sem=mr_sem.at[min(dst_dz, 8 - dst_dz)],
            device_id=column(step, 0), device_id_type=MESH,
        )
        c.start()

    def m_wait(d):
        wait_all(lmeta.at[pl.ds(0, 1 if d == 4 else 2)], mr_sem.at[d])

    def m_forward(d):
        m_wait(d)
        m_send(8 - d, 7 - d, 1)
        if d < 3:
            m_send(d, d + 1, 7)

    def sib(src, d):
        rows = src.shape[0]
        c = pltpu.make_async_remote_copy(
            src_ref=src, dst_ref=lbuf.at[pl.ds(LD * lplace(d, 1), rows)],
            send_sem=left_sem.at[2], recv_sem=sr_sem.at[d],
            device_id=column(0, 1), device_id_type=MESH,
        )
        c.start()

    def sib_forward(d):
        sib(lbuf.at[pl.ds(LD * lplace(d, 0), LD if d == 4 else 2 * LD)], d)

    def sib_wait(d):
        ref = lbuf.at[pl.ds(LD * lplace(d, 1), 2 * LD if d in (1, 2, 3) else LD)]
        pltpu.make_async_copy(ref, ref, sr_sem.at[d]).wait()

    def qrows(a, b, half):
        return qbuf.at[pl.ds(QD * qslot(a, b) + 16 * half, 16)]

    def is_last(a, b, half):
        return b == 2 or (a, b, half) in ((3, 1, 0), (3, 3, 1), (2, 1, 0), (2, 3, 1))

    def q_copy(src, dst, n, to, kind, last=False):
        c = pltpu.make_async_remote_copy(
            src_ref=src, dst_ref=dst, send_sem=left_sem.at[kind],
            recv_sem=qr_sem.at[36 if last else n], device_id=plane(to[0] % 4, to[1] % 4),
            device_id_type=MESH,
        )
        c.start()

    def q_own(a, b, to):
        for half in range(2):
            dst = qbuf.at[pl.ds(QD * qslot(a, b) + 16 * half, 16), pl.ds(0, BINS)]
            q_copy(q_in.at[pl.ds(16 * half, 16)], dst, qslot(a, b) * 2 + half, to, 3)

    EXT = ((1, 0), (3, 0), (0, 1), (0, 3))

    def ext_ref(a, b):
        return qbuf.at[pl.ds(QD * qslot(a, b), QD), pl.ds(BINS, 128)]

    def q_ext(a, b, to):
        q_copy(ext_ref(0, 0), ext_ref(a, b), 32 + EXT.index((a, b)), to, 4)

    def ext_wait(a, b):
        ref = ext_ref(a, b)
        pltpu.make_async_copy(ref, ref, qr_sem.at[32 + EXT.index((a, b))]).wait()

    def q_send(a, b, half, to):
        na, nb = (a - to[0]) % 4, (b - to[1]) % 4
        n = qslot(na, nb) * 2 + half
        q_copy(qrows(a, b, half), qrows(na, nb, half), n, to, 5, is_last(na, nb, half))

    def q_wait(a, b, half):
        rows = pl.ds(QD * qslot(a, b) + 16 * half, 16)
        ref = qbuf.at[rows, pl.ds(0, BINS)] if (a, b) in EXT else qbuf.at[rows]
        pltpu.make_async_copy(ref, ref, qr_sem.at[qslot(a, b) * 2 + half]).wait()

    for part in range(2):
        l_send(l_in.at[pl.ds(*UP[part])], 7, part, 1)
        l_send(l_in.at[pl.ds(*DOWN[part])], 1, part, 7)
    sib(l_in, 0)
    q_own(3, 0, (1, 0))
    q_own(1, 0, (3, 0))

    lane = lax.broadcasted_iota(jnp.int32, (1, 128), 1)

    def squares(ref, rows):
        acc = jnp.zeros((rows, 128), jnp.float32)
        for t in range(BINS // 128):
            v = ref[0:rows, 128 * t:128 * (t + 1)].astype(jnp.float32)
            acc = acc + v * v
        return acc

    for c in small:
        c.wait()
    loc_q.wait()
    total = jnp.sum(squares(qbuf, QD), axis=1, keepdims=True)
    qscale = lax.rsqrt(total * (1.0 / BINS) + EPS) * (1.0 / math.sqrt(BINS))
    high = qscale.astype(jnp.bfloat16).astype(jnp.float32)
    mid = (qscale - high).astype(jnp.bfloat16).astype(jnp.float32)
    rest = qscale - high - mid
    row = lax.broadcasted_iota(jnp.int32, (QD, 128), 0)
    col = lax.broadcasted_iota(jnp.int32, (QD, 128), 1)
    ext = jnp.where(row < QBLK, w_in[0], w_in[1]).astype(jnp.float32)
    for i, piece in enumerate((high, mid, rest)):
        ext = jnp.where(col == i + 1, piece, ext)
    qbuf[0:QD, BINS:WIDE] = ext.astype(jnp.bfloat16)
    q_ext(3, 0, (1, 0))
    q_ext(1, 0, (3, 0))
    q_ext(0, 3, (0, 1))
    q_ext(0, 1, (0, 3))

    loc_l.wait()
    acc = squares(lbuf, LD)
    acc = jnp.concatenate([acc, jnp.zeros((128 - LD, 128), jnp.float32)], axis=0)
    total = jnp.sum(acc.T, axis=0, keepdims=True)
    lscale = lax.rsqrt(total * (1.0 / BINS) + EPS)
    row_band = jnp.zeros((1, 128), jnp.int32)
    for j in range(LD // LBLK):
        row_band = jnp.where(lane >= 64 + LBLK * j, b_in[j], row_band)
    lmeta[0] = jnp.where(lane < 64, lscale, row_band.astype(jnp.float32))
    m_send(0, 7, 1)
    m_send(0, 1, 7)
    q_own(0, 3, (0, 1))
    q_own(0, 1, (0, 3))

    qt32[:, 0:MAXSHIFT, :] = jnp.zeros((4, MAXSHIFT, 128), jnp.float32)
    qt32[:, BINS + MAXSHIFT:PAD, :] = jnp.zeros((4, MAXSHIFT, 128), jnp.float32)

    eye_r = lax.broadcasted_iota(jnp.int32, (256, 256), 0)
    eye_c = lax.broadcasted_iota(jnp.int32, (256, 256), 1)
    eye = (eye_r == eye_c).astype(jnp.float32).astype(jnp.bfloat16)

    def prepare(tiles):
        cols = slice(128 * tiles[0], 128 * tiles[-1] + 128)

        def turned(c0, width):
            return lax.dot_general(
                eye[0:width, 0:width], qbuf[cols, c0:c0 + width],
                (((1,), (1,)), ((), ())), preferred_element_type=jnp.float32,
            )

        for c0 in range(0, BINS, 256):
            v = turned(c0, 256)
            r0 = MAXSHIFT + c0
            for i, t in enumerate(tiles):
                qt32[t, r0:r0 + 256, :] = v[:, 128 * i:128 * i + 128]
        ext = turned(BINS, 128)
        qrow[0:1, cols] = ext[1:2] + ext[2:3] + ext[3:4]
        qrow[1:2, cols] = ext[0:1]
        offs = [s_in[k] + MAXSHIFT for k in range(NOFF)]

        @pl.loop(0, BINS // 128)
        def _(i):
            r0 = pl.multiple_of(i * 128, 128)
            for k in range(NOFF):
                for t in tiles:
                    v = qt32[t, pl.ds(r0 + offs[k], 128), :]
                    qtk[k, pl.ds(r0, 128), 128 * t:128 * t + 128] = v.astype(jnp.bfloat16)

    def multiply(row, rows, h, beside=()):
        beside = list(beside)
        each = -(-len(beside) // NOFF)
        cols = slice(256 * h, 256 * h + 256)
        for k in range(NOFF):
            d = jnp.dot(
                lbuf[row:row + rows, :], qtk[k, :, cols], preferred_element_type=jnp.float32
            )
            if k:
                d = jnp.maximum(sc[row:row + rows, cols], d)
            sc[row:row + rows, cols] = d
            for f in beside[each * k:each * (k + 1)]:
                f()

    def select(g, t):
        cols = slice(128 * t, 128 * t + 128)
        scale_q = jnp.broadcast_to(qrow[0:1, cols], (8, 128))
        low = jnp.broadcast_to(qrow[1:2, cols], (8, 128))
        high = low + float(SPAN)
        vals = []
        for i in range(16):
            r = g * 128 + 8 * i
            band = lband[r:r + 8, :]
            v = sc[r:r + 8, cols] * scale_q * lsc[r:r + 8, :]
            keep = (band >= low) & (band < high)
            vals.append(jnp.where(keep, v, MASKED))
        vals = sort16(vals)
        if g:
            vals = merge16([best[t, i] for i in range(16)], vals)
        for i in range(16):
            best[t, i] = vals[i]

    def selects(groups, tiles):
        return [functools.partial(select, g, t) for g in groups for t in tiles]

    def spread(c, dz):
        m = jnp.broadcast_to(lmeta[8 * c + dz], (128, 128)).T
        r = LD * lplace(dz, c)
        lsc[r:r + LD, :] = m[0:LD]
        lband[r:r + LD, :] = m[64:64 + LD]

    def q_first(a, half):
        if half == 0:
            ext_wait(a, 0)
        q_wait(a, 0, half)
        if (a, half) == (1, 1):
            q_send(1, 0, 1, (-1, 0))
        if (a, half) == (3, 0):
            q_send(3, 0, 0, (1, 0))
        q_send(a, 0, half, (0, 1))
        q_send(a, 0, half, (0, -1))

    def q_across(half):
        q_wait(2, 0, half)
        q_send(2, 0, half, (0, 1))
        q_send(2, 0, half, (0, -1))

    def q_second(a, half):
        b = 1 if half else 3
        if a == 0:
            ext_wait(0, b)
        q_wait(a, b, half)
        q_send(a, b, half, (0, -1) if half else (0, 1))

    def q_rest(a):
        q_wait(a, 1, 0)
        q_wait(a, 3, 1)

    q_first(1, 0)
    q_first(3, 0)
    l_forward(1, 0)
    q_first(1, 1)
    m_forward(1)
    l_forward(1, 1)
    q_second(0, 1)
    q_first(3, 1)
    q_across(0)
    sib_forward(1)
    q_second(3, 0)
    q_second(0, 0)
    q_second(1, 0)
    q_across(1)
    q_second(1, 1)
    prepare((0,))
    m_forward(2)
    l_forward(2, 0)
    q_rest(0)
    q_rest(1)
    prepare((1,))
    q_second(3, 1)
    l_forward(2, 1)
    q_second(2, 0)
    sib_forward(2)
    m_forward(3)
    q_second(2, 1)
    sib_wait(0)
    sib_wait(1)
    multiply(0, 288, 0)
    sib_wait(2)
    multiply(288, 192, 0)
    l_last()
    ref = qbuf.at[pl.ds(0, 192)]
    pltpu.make_async_copy(ref, ref, qr_sem.at[36]).wait()
    prepare((2, 3))
    m_wait(4)
    pltpu.make_async_remote_copy(
        src_ref=lmeta.at[pl.ds(0, 8)], dst_ref=lmeta.at[pl.ds(8, 8)], send_sem=left_sem.at[6],
        recv_sem=mr_sem.at[0], device_id=column(0, 1), device_id_type=MESH,
    ).start()
    multiply(0, 288, 1, [functools.partial(spread, 0, dz) for dz in range(8)])
    l_wait(3, 1)
    sib_forward(3)
    pltpu.make_async_copy(lmeta.at[pl.ds(8, 8)], lmeta.at[pl.ds(8, 8)], mr_sem.at[0]).wait()
    multiply(288, 192, 1, [functools.partial(spread, 1, dz) for dz in range(8)])
    l_wait(4, 0)
    sib_forward(4)
    sib_wait(3)
    multiply(480, 192, 1, selects(range(3), (2, 3)))
    sib_wait(4)

    def finish(t):
        vals = [best[t, i] for i in range(16)]
        for sh in (4, 2, 1):
            vals = merge16(vals, [pltpu.roll(v, sh, 0) for v in vals])
        for i in range(16):
            fin[t, i:i + 1, :] = vals[i][0:1]
        for p in (3, 2, 1, 0):
            n = 4 * t + p
            if n == 0:
                continue
            a, b = SLOTS[n]
            pltpu.make_async_remote_copy(
                src_ref=fin.at[t], dst_ref=got.at[n], send_sem=f_sem.at[0],
                recv_sem=f_sem.at[1], device_id=plane(a, b), device_id_type=MESH,
            ).start()

    multiply(672, 96, 1, selects(range(3, 5), (2, 3)))
    for t in (3, 2):
        select(5, t)
        finish(t)
    multiply(480, 288, 0, selects(range(3), (0, 1)))
    for t in (1, 0):
        for g in range(3, 6):
            select(g, t)
        finish(t)
    got[0] = fin[0]
    wait_all(lbuf.at[pl.ds(0, 7 * LD)], left_sem.at[0])
    wait_all(lmeta.at[pl.ds(0, 7)], left_sem.at[1])
    wait_all(lbuf.at[pl.ds(0, 8 * LD)], left_sem.at[2])
    wait_all(lbuf.at[pl.ds(0, 4 * QD)], left_sem.at[3])
    wait_all(qbuf.at[pl.ds(0, 4 * QD), pl.ds(BINS, 128)], left_sem.at[4])
    wait_all(qbuf.at[pl.ds(0, 11 * QD)], left_sem.at[5])
    wait_all(lmeta.at[pl.ds(0, 8)], left_sem.at[6])
    pltpu.make_async_copy(got.at[pl.ds(1, 15)], got.at[pl.ds(1, 15)], f_sem.at[0]).wait()
    pltpu.make_async_copy(got.at[pl.ds(1, 15)], got.at[pl.ds(1, 15)], f_sem.at[1]).wait()

    part = lax.div(lax.broadcasted_iota(jnp.int32, (8, 128), 1), QD)
    vals = []
    for r in range(16):
        rows = []
        for t in range(4):
            v = got[4 * t, r:r + 1, :]
            for p in range(1, 4):
                v = jnp.where(part[0:1] == p, got[4 * t + p, r:r + 1, :], v)
            rows.append(v)
        vals.append(jnp.concatenate(rows + rows, axis=0))
    for sh in (2, 1):
        vals = merge16(vals, [pltpu.roll(v, sh, 0) for v in vals])
    for sh in (64, 32):
        vals = merge16(vals, [pltpu.roll(v, sh, 1) for v in vals])
    for i in range(TOPK):
        out[i:i + 1, :] = vals[i][0:1, 0:QD]


def local(queries, windows, library, bands, shifts):
    dma = pltpu.SemaphoreType.DMA
    f32, bf16 = jnp.float32, jnp.bfloat16
    hbm = pl.BlockSpec(memory_space=pltpu.HBM)
    return pl.pallas_call(
        kernel,
        out_shape=jax.ShapeDtypeStruct((TOPK, QD), f32),
        in_specs=[hbm] * 5,
        out_specs=pl.BlockSpec(memory_space=pltpu.VMEM),
        scratch_shapes=[
            pltpu.SMEM((2,), jnp.int32),
            pltpu.SMEM((6,), jnp.int32),
            pltpu.SMEM((NOFF,), jnp.int32),
            pltpu.VMEM((NQ, WIDE), bf16),
            pltpu.VMEM((NL, BINS), bf16),
            pltpu.VMEM((4, PAD, 128), f32),
            pltpu.VMEM((NOFF, BINS, NQ), bf16),
            pltpu.VMEM((NL, NQ), f32),
            pltpu.VMEM((NL, 128), f32),
            pltpu.VMEM((NL, 128), f32),
            pltpu.VMEM((8, NQ), f32),
            pltpu.VMEM((4, 16, 8, 128), f32),
            pltpu.VMEM((16, 1, 128), f32),
            pltpu.VMEM((4, 16, 128), f32),
            pltpu.VMEM((16, 16, 128), f32),
            dma((5,)), dma((7,)), dma((37,)), dma((9,)), dma((5,)), dma((5,)), dma((2,)),
        ],
        compiler_params=pltpu.CompilerParams(
            collective_id=0, has_side_effects=True, vmem_limit_bytes=62 * 2**20
        ),
        cost_estimate=pl.CostEstimate(
            flops=2 * NQ * NL * BINS * NOFF, bytes_accessed=2 * (QD + LD) * BINS, transcendentals=0
        ),
    )(queries, windows, library, bands, shifts).T


def solution(mesh):
    return jax.shard_map(
        local,
        mesh=mesh,
        in_specs=(
            P(("blk", "grp"), None),
            P(("blk", "grp")),
            P(("blk", "grp"), None),
            P(("blk", "grp")),
            P(),
        ),
        out_specs=P(("blk", "grp"), None),
        check_vma=False,
    )
```

```python
import functools
import math

import jax
import jax.numpy as jnp
from jax import lax
from jax.experimental import pallas as pl
from jax.experimental.pallas import tpu as pltpu
from jax.sharding import PartitionSpec as P

BINS = 2048
NOFF = 4
TOPK = 16
MAXSHIFT = 24
QBLK = 16
LBLK = 8
SPAN = 4
EPS = 1e-06
MASKED = -8.0

QD = 32
LD = 48
CH = 16
NQ = 16 * QD
NL = 16 * LD
PAD = BINS + 2 * MAXSHIFT
WIDE = BINS + 128
MESH = pl.DeviceIdType.MESH

SLOTS = [
    (0, 0), (1, 0), (3, 0), (2, 0),
    (0, 1), (0, 3), (1, 1), (1, 3),
    (3, 1), (3, 3), (2, 1), (2, 3),
    (0, 2), (1, 2), (3, 2), (2, 2),
]


def qslot(a, b):
    return SLOTS.index((a % 4, b % 4))


def lplace(dz, c):
    dz %= 8
    if dz == 0:
        return c
    if dz == 4:
        return 14 + c
    d = min(dz, 8 - dz)
    return 2 + 4 * (d - 1) + 2 * c + (1 if dz > 4 else 0)


def batcher(n):
    pairs = []
    p = 1
    while p < n:
        k = p
        while k >= 1:
            for j in range(k % p, n - k, 2 * k):
                for i in range(min(k, n - j - k)):
                    if (i + j) // (2 * p) == (i + j + k) // (2 * p):
                        pairs.append((i + j, i + j + k))
            k //= 2
        p *= 2
    return pairs


SORT16 = batcher(16)


def sort16(v):
    v = list(v)
    for i, j in SORT16:
        v[i], v[j] = jnp.maximum(v[i], v[j]), jnp.minimum(v[i], v[j])
    return v


def merge16(a, b):
    v = [jnp.maximum(a[i], b[15 - i]) for i in range(16)]
    for d in (8, 4, 2, 1):
        for i in range(16):
            if not i & d:
                v[i], v[i + d] = jnp.maximum(v[i], v[i + d]), jnp.minimum(v[i], v[i + d])
    return v


def kernel(
    q_in, w_hbm, l_in, b_hbm, s_hbm, out,
    w_in, b_in, s_in, qbuf, lbuf, qt32, qtk, sc, lsc, lband, qrow, best, lmeta, fin, got,
    loc_sem, left_sem, qr_sem, lr_sem, sr_sem, mr_sem, f_sem,
):
    blk = lax.axis_index("blk")
    grp = lax.axis_index("grp")
    core = lax.rem(blk, 2)
    z = lax.rem(lax.div(blk, 2), 8)
    x = lax.div(grp, 2)
    y = lax.rem(grp, 2) * 2 + lax.div(blk, 16)

    def place(px, py, pz, pc):
        return {
            "blk": (lax.rem(py, 2) * 8 + pz) * 2 + pc,
            "grp": px * 2 + lax.div(py, 2),
        }

    def plane(a, b):
        dx = a * (1 - core) + b * core
        dy = b * (1 - core) + a * core
        return place(lax.rem(x + dx, 4), lax.rem(y + dy, 4), z, core)

    def column(dz, dc):
        return place(x, y, lax.rem(z + dz, 8), core + dc * (1 - 2 * core))

    barrier = pltpu.get_barrier_semaphore()
    near = [plane(1, 0), plane(3, 0), plane(0, 1), plane(0, 3)]
    near += [column(1, 0), column(7, 0), column(0, 1)]
    for peer in near:
        pl.semaphore_signal(barrier, inc=1, device_id=peer, device_id_type=MESH)
    loc_q = pltpu.make_async_copy(q_in, qbuf.at[pl.ds(0, QD), pl.ds(0, BINS)], loc_sem.at[0])
    loc_l = pltpu.make_async_copy(l_in, lbuf.at[pl.ds(0, LD)], loc_sem.at[1])
    loc_q.start()
    loc_l.start()
    small = [
        pltpu.make_async_copy(src, dst, loc_sem.at[2 + i])
        for i, (src, dst) in enumerate(((w_hbm, w_in), (b_hbm, b_in), (s_hbm, s_in)))
    ]
    for c in small:
        c.start()
    pl.semaphore_wait(barrier, len(near))

    def wait_all(ref, sem):
        pltpu.make_async_copy(ref, ref, sem).wait()

    UP = ((0, 32), (32, 16))
    DOWN = ((16, 32), (0, 16))

    def lrows(dz, part):
        if dz == 4:
            return lbuf.at[pl.ds(LD * lplace(4, 0), LD)]
        r, n = (UP if dz > 4 else DOWN)[part]
        return lbuf.at[pl.ds(LD * lplace(dz, 0) + r, n)]

    def l_copy(src, dst, n, step):
        c = pltpu.make_async_remote_copy(
            src_ref=src, dst_ref=dst, send_sem=left_sem.at[0],
            recv_sem=lr_sem.at[n], device_id=column(step, 0), device_id_type=MESH,
        )
        c.start()

    def l_send(src, dz, part, step):
        l_copy(src, lrows(dz, part), 2 * min(dz, 8 - dz) + part, step)

    def l_wait(d, part):
        wait_all(lbuf.at[pl.ds(0, LD if d == 4 else (64, 32)[part])], lr_sem.at[2 * d + part])

    def l_forward(d, part):
        l_wait(d, part)
        l_send(lrows(8 - d, part), 7 - d, part, 1)
        l_send(lrows(d, part), d + 1, part, 7)

    def l_last():
        l_wait(3, 0)
        up, down, far = (LD * lplace(dz, 0) for dz in (5, 3, 4))
        mid = up * (1 - core) + down * core + CH
        for src, r, step in (
            (up, 0, 1), (down + 2 * CH, 2 * CH, 7), (mid, CH, 1 + 6 * core)
        ):
            src = lbuf.at[pl.ds(pl.multiple_of(src, CH), CH)]
            l_copy(src, lbuf.at[pl.ds(far + r, CH)], 8, step)

    def m_send(src_dz, dst_dz, step):
        c = pltpu.make_async_remote_copy(
            src_ref=lmeta.at[src_dz], dst_ref=lmeta.at[dst_dz],
            send_sem=left_sem.at[1], recv_sem=mr_sem.at[min(dst_dz, 8 - dst_dz)],
            device_id=column(step, 0), device_id_type=MESH,
        )
        c.start()

    def m_wait(d):
        wait_all(lmeta.at[pl.ds(0, 1 if d == 4 else 2)], mr_sem.at[d])

    def m_forward(d):
        m_wait(d)
        m_send(8 - d, 7 - d, 1)
        if d < 3:
            m_send(d, d + 1, 7)

    def sib(src, d):
        rows = src.shape[0]
        c = pltpu.make_async_remote_copy(
            src_ref=src, dst_ref=lbuf.at[pl.ds(LD * lplace(d, 1), rows)],
            send_sem=left_sem.at[2], recv_sem=sr_sem.at[d],
            device_id=column(0, 1), device_id_type=MESH,
        )
        c.start()

    def sib_forward(d):
        sib(lbuf.at[pl.ds(LD * lplace(d, 0), LD if d == 4 else 2 * LD)], d)

    def sib_wait(d):
        ref = lbuf.at[pl.ds(LD * lplace(d, 1), 2 * LD if d in (1, 2, 3) else LD)]
        pltpu.make_async_copy(ref, ref, sr_sem.at[d]).wait()

    def qrows(a, b, half):
        return qbuf.at[pl.ds(QD * qslot(a, b) + 16 * half, 16)]

    def is_last(a, b, half):
        return b == 2 or (a, b, half) in ((3, 1, 0), (3, 3, 1), (2, 1, 0), (2, 3, 1))

    def q_copy(src, dst, n, to, kind, last=False):
        c = pltpu.make_async_remote_copy(
            src_ref=src, dst_ref=dst, send_sem=left_sem.at[kind],
            recv_sem=qr_sem.at[36 if last else n], device_id=plane(to[0] % 4, to[1] % 4),
            device_id_type=MESH,
        )
        c.start()

    def q_own(a, b, to):
        for half in range(2):
            dst = qbuf.at[pl.ds(QD * qslot(a, b) + 16 * half, 16), pl.ds(0, BINS)]
            q_copy(q_in.at[pl.ds(16 * half, 16)], dst, qslot(a, b) * 2 + half, to, 3)

    EXT = ((1, 0), (3, 0), (0, 1), (0, 3))

    def ext_ref(a, b):
        return qbuf.at[pl.ds(QD * qslot(a, b), QD), pl.ds(BINS, 128)]

    def q_ext(a, b, to):
        q_copy(ext_ref(0, 0), ext_ref(a, b), 32 + EXT.index((a, b)), to, 4)

    def ext_wait(a, b):
        ref = ext_ref(a, b)
        pltpu.make_async_copy(ref, ref, qr_sem.at[32 + EXT.index((a, b))]).wait()

    def q_send(a, b, half, to):
        na, nb = (a - to[0]) % 4, (b - to[1]) % 4
        n = qslot(na, nb) * 2 + half
        q_copy(qrows(a, b, half), qrows(na, nb, half), n, to, 5, is_last(na, nb, half))

    def q_wait(a, b, half):
        rows = pl.ds(QD * qslot(a, b) + 16 * half, 16)
        ref = qbuf.at[rows, pl.ds(0, BINS)] if (a, b) in EXT else qbuf.at[rows]
        pltpu.make_async_copy(ref, ref, qr_sem.at[qslot(a, b) * 2 + half]).wait()

    for part in range(2):
        l_send(l_in.at[pl.ds(*UP[part])], 7, part, 1)
        l_send(l_in.at[pl.ds(*DOWN[part])], 1, part, 7)
    sib(l_in, 0)
    q_own(3, 0, (1, 0))
    q_own(1, 0, (3, 0))

    lane = lax.broadcasted_iota(jnp.int32, (1, 128), 1)

    def squares(ref, rows):
        acc = jnp.zeros((rows, 128), jnp.float32)
        for t in range(BINS // 128):
            v = ref[0:rows, 128 * t:128 * (t + 1)].astype(jnp.float32)
            acc = acc + v * v
        return acc

    for c in small:
        c.wait()
    loc_q.wait()
    total = jnp.sum(squares(qbuf, QD), axis=1, keepdims=True)
    qscale = lax.rsqrt(total * (1.0 / BINS) + EPS) * (1.0 / math.sqrt(BINS))
    high = qscale.astype(jnp.bfloat16).astype(jnp.float32)
    mid = (qscale - high).astype(jnp.bfloat16).astype(jnp.float32)
    rest = qscale - high - mid
    row = lax.broadcasted_iota(jnp.int32, (QD, 128), 0)
    col = lax.broadcasted_iota(jnp.int32, (QD, 128), 1)
    ext = jnp.where(row < QBLK, w_in[0], w_in[1]).astype(jnp.float32)
    for i, piece in enumerate((high, mid, rest)):
        ext = jnp.where(col == i + 1, piece, ext)
    qbuf[0:QD, BINS:WIDE] = ext.astype(jnp.bfloat16)
    q_ext(3, 0, (1, 0))
    q_ext(1, 0, (3, 0))
    q_ext(0, 3, (0, 1))
    q_ext(0, 1, (0, 3))

    loc_l.wait()
    acc = squares(lbuf, LD)
    acc = jnp.concatenate([acc, jnp.zeros((128 - LD, 128), jnp.float32)], axis=0)
    total = jnp.sum(acc.T, axis=0, keepdims=True)
    lscale = lax.rsqrt(total * (1.0 / BINS) + EPS)
    row_band = jnp.zeros((1, 128), jnp.int32)
    for j in range(LD // LBLK):
        row_band = jnp.where(lane >= 64 + LBLK * j, b_in[j], row_band)
    lmeta[0] = jnp.where(lane < 64, lscale, row_band.astype(jnp.float32))
    m_send(0, 7, 1)
    m_send(0, 1, 7)
    q_own(0, 3, (0, 1))
    q_own(0, 1, (0, 3))

    qt32[:, 0:MAXSHIFT, :] = jnp.zeros((4, MAXSHIFT, 128), jnp.float32)
    qt32[:, BINS + MAXSHIFT:PAD, :] = jnp.zeros((4, MAXSHIFT, 128), jnp.float32)

    eye_r = lax.broadcasted_iota(jnp.int32, (256, 256), 0)
    eye_c = lax.broadcasted_iota(jnp.int32, (256, 256), 1)
    eye = (eye_r == eye_c).astype(jnp.float32).astype(jnp.bfloat16)

    def prepare(tiles):
        cols = slice(128 * tiles[0], 128 * tiles[-1] + 128)

        def turned(c0, width):
            return lax.dot_general(
                eye[0:width, 0:width], qbuf[cols, c0:c0 + width],
                (((1,), (1,)), ((), ())), preferred_element_type=jnp.float32,
            )

        for c0 in range(0, BINS, 256):
            v = turned(c0, 256)
            r0 = MAXSHIFT + c0
            for i, t in enumerate(tiles):
                qt32[t, r0:r0 + 256, :] = v[:, 128 * i:128 * i + 128]
        ext = turned(BINS, 128)
        qrow[0:1, cols] = ext[1:2] + ext[2:3] + ext[3:4]
        qrow[1:2, cols] = ext[0:1]
        offs = [s_in[k] + MAXSHIFT for k in range(NOFF)]

        @pl.loop(0, BINS // 128)
        def _(i):
            r0 = pl.multiple_of(i * 128, 128)
            for k in range(NOFF):
                for t in tiles:
                    v = qt32[t, pl.ds(r0 + offs[k], 128), :]
                    qtk[k, pl.ds(r0, 128), 128 * t:128 * t + 128] = v.astype(jnp.bfloat16)

    def multiply(row, rows, h, beside=()):
        beside = list(beside)
        each = -(-len(beside) // NOFF)
        cols = slice(256 * h, 256 * h + 256)
        for k in range(NOFF):
            d = jnp.dot(
                lbuf[row:row + rows, :], qtk[k, :, cols], preferred_element_type=jnp.float32
            )
            if k:
                d = jnp.maximum(sc[row:row + rows, cols], d)
            sc[row:row + rows, cols] = d
            for f in beside[each * k:each * (k + 1)]:
                f()

    def select(g, t):
        cols = slice(128 * t, 128 * t + 128)
        scale_q = jnp.broadcast_to(qrow[0:1, cols], (8, 128))
        low = jnp.broadcast_to(qrow[1:2, cols], (8, 128))
        high = low + float(SPAN)
        vals = []
        for i in range(16):
            r = g * 128 + 8 * i
            band = lband[r:r + 8, :]
            v = sc[r:r + 8, cols] * scale_q * lsc[r:r + 8, :]
            keep = (band >= low) & (band < high)
            vals.append(jnp.where(keep, v, MASKED))
        vals = sort16(vals)
        if g:
            vals = merge16([best[t, i] for i in range(16)], vals)
        for i in range(16):
            best[t, i] = vals[i]

    def selects(groups, tiles):
        return [functools.partial(select, g, t) for g in groups for t in tiles]

    def spread(c, dz):
        m = jnp.broadcast_to(lmeta[8 * c + dz], (128, 128)).T
        r = LD * lplace(dz, c)
        lsc[r:r + LD, :] = m[0:LD]
        lband[r:r + LD, :] = m[64:64 + LD]

    def q_first(a, half):
        if half == 0:
            ext_wait(a, 0)
        q_wait(a, 0, half)
        if (a, half) == (1, 1):
            q_send(1, 0, 1, (-1, 0))
        if (a, half) == (3, 0):
            q_send(3, 0, 0, (1, 0))
        q_send(a, 0, half, (0, 1))
        q_send(a, 0, half, (0, -1))

    def q_across(half):
        q_wait(2, 0, half)
        q_send(2, 0, half, (0, 1))
        q_send(2, 0, half, (0, -1))

    def q_second(a, half):
        b = 1 if half else 3
        if a == 0:
            ext_wait(0, b)
        q_wait(a, b, half)
        q_send(a, b, half, (0, -1) if half else (0, 1))

    def q_rest(a):
        q_wait(a, 1, 0)
        q_wait(a, 3, 1)

    q_first(1, 0)
    q_first(3, 0)
    l_forward(1, 0)
    q_first(1, 1)
    m_forward(1)
    l_forward(1, 1)
    q_second(0, 1)
    q_first(3, 1)
    q_across(0)
    sib_forward(1)
    q_second(3, 0)
    q_second(0, 0)
    q_second(1, 0)
    q_across(1)
    q_second(1, 1)
    prepare((0,))
    m_forward(2)
    l_forward(2, 0)
    q_rest(0)
    q_rest(1)
    prepare((1,))
    q_second(3, 1)
    l_forward(2, 1)
    q_second(2, 0)
    sib_forward(2)
    m_forward(3)
    q_second(2, 1)
    sib_wait(0)
    sib_wait(1)
    multiply(0, 288, 0)
    l_last()
    sib_wait(2)
    multiply(288, 192, 0)
    ref = qbuf.at[pl.ds(0, 192)]
    pltpu.make_async_copy(ref, ref, qr_sem.at[36]).wait()
    prepare((2, 3))
    m_wait(4)
    pltpu.make_async_remote_copy(
        src_ref=lmeta.at[pl.ds(0, 8)], dst_ref=lmeta.at[pl.ds(8, 8)], send_sem=left_sem.at[6],
        recv_sem=mr_sem.at[0], device_id=column(0, 1), device_id_type=MESH,
    ).start()
    multiply(0, 288, 1, [functools.partial(spread, 0, dz) for dz in range(8)])
    l_wait(3, 1)
    sib_forward(3)
    l_wait(4, 0)
    sib_forward(4)
    pltpu.make_async_copy(lmeta.at[pl.ds(8, 8)], lmeta.at[pl.ds(8, 8)], mr_sem.at[0]).wait()
    multiply(288, 192, 1, [functools.partial(spread, 1, dz) for dz in range(8)])
    sib_wait(3)
    sib_wait(4)

    def finish(t):
        vals = [best[t, i] for i in range(16)]
        for sh in (4, 2, 1):
            vals = merge16(vals, [pltpu.roll(v, sh, 0) for v in vals])
        for i in range(16):
            fin[t, i:i + 1, :] = vals[i][0:1]
        for p in (3, 2, 1, 0):
            n = 4 * t + p
            if n == 0:
                continue
            a, b = SLOTS[n]
            pltpu.make_async_remote_copy(
                src_ref=fin.at[t], dst_ref=got.at[n], send_sem=f_sem.at[0],
                recv_sem=f_sem.at[1], device_id=plane(a, b), device_id_type=MESH,
            ).start()

    for tiles in ((3, 2), (1, 0)):
        multiply(480, 288, tiles[1] // 2, selects(range(3), tiles))
        for t in tiles:
            for g in range(3, 6):
                select(g, t)
            finish(t)
    got[0] = fin[0]
    wait_all(lbuf.at[pl.ds(0, 7 * LD)], left_sem.at[0])
    wait_all(lmeta.at[pl.ds(0, 7)], left_sem.at[1])
    wait_all(lbuf.at[pl.ds(0, 8 * LD)], left_sem.at[2])
    wait_all(lbuf.at[pl.ds(0, 4 * QD)], left_sem.at[3])
    wait_all(qbuf.at[pl.ds(0, 4 * QD), pl.ds(BINS, 128)], left_sem.at[4])
    wait_all(qbuf.at[pl.ds(0, 11 * QD)], left_sem.at[5])
    wait_all(lmeta.at[pl.ds(0, 8)], left_sem.at[6])
    pltpu.make_async_copy(got.at[pl.ds(1, 15)], got.at[pl.ds(1, 15)], f_sem.at[0]).wait()
    pltpu.make_async_copy(got.at[pl.ds(1, 15)], got.at[pl.ds(1, 15)], f_sem.at[1]).wait()

    part = lax.div(lax.broadcasted_iota(jnp.int32, (8, 128), 1), QD)
    vals = []
    for r in range(16):
        rows = []
        for t in range(4):
            v = got[4 * t, r:r + 1, :]
            for p in range(1, 4):
                v = jnp.where(part[0:1] == p, got[4 * t + p, r:r + 1, :], v)
            rows.append(v)
        vals.append(jnp.concatenate(rows + rows, axis=0))
    for sh in (2, 1):
        vals = merge16(vals, [pltpu.roll(v, sh, 0) for v in vals])
    for sh in (64, 32):
        vals = merge16(vals, [pltpu.roll(v, sh, 1) for v in vals])
    for i in range(TOPK):
        out[i:i + 1, :] = vals[i][0:1, 0:QD]


def local(queries, windows, library, bands, shifts):
    dma = pltpu.SemaphoreType.DMA
    f32, bf16 = jnp.float32, jnp.bfloat16
    hbm = pl.BlockSpec(memory_space=pltpu.HBM)
    return pl.pallas_call(
        kernel,
        out_shape=jax.ShapeDtypeStruct((TOPK, QD), f32),
        in_specs=[hbm] * 5,
        out_specs=pl.BlockSpec(memory_space=pltpu.VMEM),
        scratch_shapes=[
            pltpu.SMEM((2,), jnp.int32),
            pltpu.SMEM((6,), jnp.int32),
            pltpu.SMEM((NOFF,), jnp.int32),
            pltpu.VMEM((NQ, WIDE), bf16),
            pltpu.VMEM((NL, BINS), bf16),
            pltpu.VMEM((4, PAD, 128), f32),
            pltpu.VMEM((NOFF, BINS, NQ), bf16),
            pltpu.VMEM((NL, NQ), f32),
            pltpu.VMEM((NL, 128), f32),
            pltpu.VMEM((NL, 128), f32),
            pltpu.VMEM((8, NQ), f32),
            pltpu.VMEM((4, 16, 8, 128), f32),
            pltpu.VMEM((16, 1, 128), f32),
            pltpu.VMEM((4, 16, 128), f32),
            pltpu.VMEM((16, 16, 128), f32),
            dma((5,)), dma((7,)), dma((37,)), dma((9,)), dma((5,)), dma((5,)), dma((2,)),
        ],
        compiler_params=pltpu.CompilerParams(
            collective_id=0, has_side_effects=True, vmem_limit_bytes=62 * 2**20
        ),
        cost_estimate=pl.CostEstimate(
            flops=2 * NQ * NL * BINS * NOFF, bytes_accessed=2 * (QD + LD) * BINS, transcendentals=0
        ),
    )(queries, windows, library, bands, shifts).T


def solution(mesh):
    return jax.shard_map(
        local,
        mesh=mesh,
        in_specs=(
            P(("blk", "grp"), None),
            P(("blk", "grp")),
            P(("blk", "grp"), None),
            P(("blk", "grp")),
            P(),
        ),
        out_specs=P(("blk", "grp"), None),
        check_vma=False,
    )
```

```python
import functools
import math

import jax
import jax.numpy as jnp
from jax import lax
from jax.experimental import pallas as pl
from jax.experimental.pallas import tpu as pltpu
from jax.sharding import PartitionSpec as P

BINS = 2048
NOFF = 4
TOPK = 16
MAXSHIFT = 24
QBLK = 16
LBLK = 8
SPAN = 4
EPS = 1e-06
MASKED = -8.0

QD = 32
LD = 48
CH = 16
NQ = 16 * QD
NL = 16 * LD
PAD = BINS + 2 * MAXSHIFT
WIDE = BINS + 128
MESH = pl.DeviceIdType.MESH

SLOTS = [
    (0, 0), (1, 0), (3, 0), (2, 0),
    (0, 1), (0, 3), (1, 1), (1, 3),
    (3, 1), (3, 3), (2, 1), (2, 3),
    (0, 2), (1, 2), (3, 2), (2, 2),
]


def qslot(a, b):
    return SLOTS.index((a % 4, b % 4))


def lplace(dz, c):
    dz %= 8
    if dz == 0:
        return c
    if dz == 4:
        return 14 + c
    d = min(dz, 8 - dz)
    return 2 + 4 * (d - 1) + 2 * c + (1 if dz > 4 else 0)


def batcher(n):
    pairs = []
    p = 1
    while p < n:
        k = p
        while k >= 1:
            for j in range(k % p, n - k, 2 * k):
                for i in range(min(k, n - j - k)):
                    if (i + j) // (2 * p) == (i + j + k) // (2 * p):
                        pairs.append((i + j, i + j + k))
            k //= 2
        p *= 2
    return pairs


SORT16 = batcher(16)


def sort16(v):
    v = list(v)
    for i, j in SORT16:
        v[i], v[j] = jnp.maximum(v[i], v[j]), jnp.minimum(v[i], v[j])
    return v


def merge16(a, b):
    v = [jnp.maximum(a[i], b[15 - i]) for i in range(16)]
    for d in (8, 4, 2, 1):
        for i in range(16):
            if not i & d:
                v[i], v[i + d] = jnp.maximum(v[i], v[i + d]), jnp.minimum(v[i], v[i + d])
    return v


def kernel(
    q_in, w_hbm, l_in, b_hbm, s_hbm, out,
    w_in, b_in, s_in, qbuf, lbuf, qt32, qtk, sc, lsc, lband, qrow, best, lmeta, fin, got,
    loc_sem, left_sem, qr_sem, lr_sem, sr_sem, mr_sem, f_sem,
):
    blk = lax.axis_index("blk")
    grp = lax.axis_index("grp")
    core = lax.rem(blk, 2)
    z = lax.rem(lax.div(blk, 2), 8)
    x = lax.div(grp, 2)
    y = lax.rem(grp, 2) * 2 + lax.div(blk, 16)

    def place(px, py, pz, pc):
        return {
            "blk": (lax.rem(py, 2) * 8 + pz) * 2 + pc,
            "grp": px * 2 + lax.div(py, 2),
        }

    def plane(a, b):
        dx = a * (1 - core) + b * core
        dy = b * (1 - core) + a * core
        return place(lax.rem(x + dx, 4), lax.rem(y + dy, 4), z, core)

    def column(dz, dc):
        return place(x, y, lax.rem(z + dz, 8), core + dc * (1 - 2 * core))

    barrier = pltpu.get_barrier_semaphore()
    near = [plane(1, 0), plane(3, 0), plane(0, 1), plane(0, 3)]
    near += [column(1, 0), column(7, 0), column(0, 1)]
    for peer in near:
        pl.semaphore_signal(barrier, inc=1, device_id=peer, device_id_type=MESH)
    loc_q = pltpu.make_async_copy(q_in, qbuf.at[pl.ds(0, QD), pl.ds(0, BINS)], loc_sem.at[0])
    loc_l = pltpu.make_async_copy(l_in, lbuf.at[pl.ds(0, LD)], loc_sem.at[1])
    loc_q.start()
    loc_l.start()
    small = [
        pltpu.make_async_copy(src, dst, loc_sem.at[2 + i])
        for i, (src, dst) in enumerate(((w_hbm, w_in), (b_hbm, b_in), (s_hbm, s_in)))
    ]
    for c in small:
        c.start()
    pl.semaphore_wait(barrier, len(near))

    def wait_all(ref, sem):
        pltpu.make_async_copy(ref, ref, sem).wait()

    UP = ((0, 32), (32, 16))
    DOWN = ((16, 32), (0, 16))

    def lrows(dz, part):
        if dz == 4:
            return lbuf.at[pl.ds(LD * lplace(4, 0), LD)]
        r, n = (UP if dz > 4 else DOWN)[part]
        return lbuf.at[pl.ds(LD * lplace(dz, 0) + r, n)]

    def l_copy(src, dst, n, step):
        c = pltpu.make_async_remote_copy(
            src_ref=src, dst_ref=dst, send_sem=left_sem.at[0],
            recv_sem=lr_sem.at[n], device_id=column(step, 0), device_id_type=MESH,
        )
        c.start()

    def l_send(src, dz, part, step):
        l_copy(src, lrows(dz, part), 2 * min(dz, 8 - dz) + part, step)

    def l_wait(d, part):
        wait_all(lbuf.at[pl.ds(0, LD if d == 4 else (64, 32)[part])], lr_sem.at[2 * d + part])

    def l_forward(d, part):
        l_wait(d, part)
        l_send(lrows(8 - d, part), 7 - d, part, 1)
        l_send(lrows(d, part), d + 1, part, 7)

    def l_last():
        l_wait(3, 0)
        up, down, far = (LD * lplace(dz, 0) for dz in (5, 3, 4))
        mid = up * (1 - core) + down * core + CH
        for src, r, step in (
            (up, 0, 1), (down + 2 * CH, 2 * CH, 7), (mid, CH, 1 + 6 * core)
        ):
            src = lbuf.at[pl.ds(pl.multiple_of(src, CH), CH)]
            l_copy(src, lbuf.at[pl.ds(far + r, CH)], 8, step)

    def m_send(src_dz, dst_dz, step):
        c = pltpu.make_async_remote_copy(
            src_ref=lmeta.at[src_dz], dst_ref=lmeta.at[dst_dz],
            send_sem=left_sem.at[1], recv_sem=mr_sem.at[min(dst_dz, 8 - dst_dz)],
            device_id=column(step, 0), device_id_type=MESH,
        )
        c.start()

    def m_wait(d):
        wait_all(lmeta.at[pl.ds(0, 1 if d == 4 else 2)], mr_sem.at[d])

    def m_forward(d):
        m_wait(d)
        m_send(8 - d, 7 - d, 1)
        if d < 3:
            m_send(d, d + 1, 7)

    def sib(src, d):
        rows = src.shape[0]
        c = pltpu.make_async_remote_copy(
            src_ref=src, dst_ref=lbuf.at[pl.ds(LD * lplace(d, 1), rows)],
            send_sem=left_sem.at[2], recv_sem=sr_sem.at[d],
            device_id=column(0, 1), device_id_type=MESH,
        )
        c.start()

    def sib_forward(d):
        sib(lbuf.at[pl.ds(LD * lplace(d, 0), LD if d == 4 else 2 * LD)], d)

    def sib_wait(d):
        ref = lbuf.at[pl.ds(LD * lplace(d, 1), 2 * LD if d in (1, 2, 3) else LD)]
        pltpu.make_async_copy(ref, ref, sr_sem.at[d]).wait()

    def qrows(a, b, half):
        return qbuf.at[pl.ds(QD * qslot(a, b) + 16 * half, 16)]

    def arrival(a, b, half):
        if b == 2:
            return 36
        if (a, b, half) in ((3, 1, 0), (3, 3, 1), (2, 1, 0), (2, 3, 1)):
            return 37
        return qslot(a, b) * 2 + half

    def q_copy(src, dst, n, to, kind):
        c = pltpu.make_async_remote_copy(
            src_ref=src, dst_ref=dst, send_sem=left_sem.at[kind],
            recv_sem=qr_sem.at[n], device_id=plane(to[0] % 4, to[1] % 4),
            device_id_type=MESH,
        )
        c.start()

    def q_own(a, b, to):
        for half in range(2):
            dst = qbuf.at[pl.ds(QD * qslot(a, b) + 16 * half, 16), pl.ds(0, BINS)]
            q_copy(q_in.at[pl.ds(16 * half, 16)], dst, qslot(a, b) * 2 + half, to, 3)

    EXT = ((1, 0), (3, 0), (0, 1), (0, 3))

    def ext_ref(a, b):
        return qbuf.at[pl.ds(QD * qslot(a, b), QD), pl.ds(BINS, 128)]

    def q_ext(a, b, to):
        q_copy(ext_ref(0, 0), ext_ref(a, b), 32 + EXT.index((a, b)), to, 4)

    def ext_wait(a, b):
        ref = ext_ref(a, b)
        pltpu.make_async_copy(ref, ref, qr_sem.at[32 + EXT.index((a, b))]).wait()

    def q_send(a, b, half, to):
        na, nb = (a - to[0]) % 4, (b - to[1]) % 4
        q_copy(qrows(a, b, half), qrows(na, nb, half), arrival(na, nb, half), to, 5)

    def q_wait(a, b, half):
        rows = pl.ds(QD * qslot(a, b) + 16 * half, 16)
        ref = qbuf.at[rows, pl.ds(0, BINS)] if (a, b) in EXT else qbuf.at[rows]
        pltpu.make_async_copy(ref, ref, qr_sem.at[qslot(a, b) * 2 + half]).wait()

    for part in range(2):
        l_send(l_in.at[pl.ds(*UP[part])], 7, part, 1)
        l_send(l_in.at[pl.ds(*DOWN[part])], 1, part, 7)
    sib(l_in, 0)
    q_own(3, 0, (1, 0))
    q_own(1, 0, (3, 0))

    lane = lax.broadcasted_iota(jnp.int32, (1, 128), 1)

    def squares(ref, rows):
        acc = jnp.zeros((rows, 128), jnp.float32)
        for t in range(BINS // 128):
            v = ref[0:rows, 128 * t:128 * (t + 1)].astype(jnp.float32)
            acc = acc + v * v
        return acc

    for c in small:
        c.wait()
    loc_q.wait()
    total = jnp.sum(squares(qbuf, QD), axis=1, keepdims=True)
    qscale = lax.rsqrt(total * (1.0 / BINS) + EPS) * (1.0 / math.sqrt(BINS))
    high = qscale.astype(jnp.bfloat16).astype(jnp.float32)
    mid = (qscale - high).astype(jnp.bfloat16).astype(jnp.float32)
    rest = qscale - high - mid
    row = lax.broadcasted_iota(jnp.int32, (QD, 128), 0)
    col = lax.broadcasted_iota(jnp.int32, (QD, 128), 1)
    ext = jnp.where(row < QBLK, w_in[0], w_in[1]).astype(jnp.float32)
    for i, piece in enumerate((high, mid, rest)):
        ext = jnp.where(col == i + 1, piece, ext)
    qbuf[0:QD, BINS:WIDE] = ext.astype(jnp.bfloat16)
    q_ext(3, 0, (1, 0))
    q_ext(1, 0, (3, 0))
    q_ext(0, 3, (0, 1))
    q_ext(0, 1, (0, 3))

    loc_l.wait()
    acc = squares(lbuf, LD)
    acc = jnp.concatenate([acc, jnp.zeros((128 - LD, 128), jnp.float32)], axis=0)
    total = jnp.sum(acc.T, axis=0, keepdims=True)
    lscale = lax.rsqrt(total * (1.0 / BINS) + EPS)
    row_band = jnp.zeros((1, 128), jnp.int32)
    for j in range(LD // LBLK):
        row_band = jnp.where(lane >= 64 + LBLK * j, b_in[j], row_band)
    lmeta[0] = jnp.where(lane < 64, lscale, row_band.astype(jnp.float32))
    m_send(0, 7, 1)
    m_send(0, 1, 7)
    q_own(0, 3, (0, 1))
    q_own(0, 1, (0, 3))

    qt32[:, 0:MAXSHIFT, :] = jnp.zeros((4, MAXSHIFT, 128), jnp.float32)
    qt32[:, BINS + MAXSHIFT:PAD, :] = jnp.zeros((4, MAXSHIFT, 128), jnp.float32)

    eye_r = lax.broadcasted_iota(jnp.int32, (256, 256), 0)
    eye_c = lax.broadcasted_iota(jnp.int32, (256, 256), 1)
    eye = (eye_r == eye_c).astype(jnp.float32).astype(jnp.bfloat16)

    def prepare(tiles):
        cols = slice(128 * tiles[0], 128 * tiles[-1] + 128)

        def turned(c0, width):
            return lax.dot_general(
                eye[0:width, 0:width], qbuf[cols, c0:c0 + width],
                (((1,), (1,)), ((), ())), preferred_element_type=jnp.float32,
            )

        for c0 in range(0, BINS, 256):
            v = turned(c0, 256)
            r0 = MAXSHIFT + c0
            for i, t in enumerate(tiles):
                qt32[t, r0:r0 + 256, :] = v[:, 128 * i:128 * i + 128]
        ext = turned(BINS, 128)
        qrow[0:1, cols] = ext[1:2] + ext[2:3] + ext[3:4]
        qrow[1:2, cols] = ext[0:1]
        offs = [s_in[k] + MAXSHIFT for k in range(NOFF)]

        @pl.loop(0, BINS // 128)
        def _(i):
            r0 = pl.multiple_of(i * 128, 128)
            for k in range(NOFF):
                for t in tiles:
                    v = qt32[t, pl.ds(r0 + offs[k], 128), :]
                    qtk[k, pl.ds(r0, 128), 128 * t:128 * t + 128] = v.astype(jnp.bfloat16)

    def multiply(row, rows, h, beside=()):
        beside = list(beside)
        each = -(-len(beside) // NOFF)
        cols = slice(256 * h, 256 * h + 256)
        for k in range(NOFF):
            d = jnp.dot(
                lbuf[row:row + rows, :], qtk[k, :, cols], preferred_element_type=jnp.float32
            )
            if k:
                d = jnp.maximum(sc[row:row + rows, cols], d)
            sc[row:row + rows, cols] = d
            for f in beside[each * k:each * (k + 1)]:
                f()

    def select(g, t):
        cols = slice(128 * t, 128 * t + 128)
        scale_q = jnp.broadcast_to(qrow[0:1, cols], (8, 128))
        low = jnp.broadcast_to(qrow[1:2, cols], (8, 128))
        high = low + float(SPAN)
        vals = []
        for i in range(16):
            r = g * 128 + 8 * i
            band = lband[r:r + 8, :]
            v = sc[r:r + 8, cols] * scale_q * lsc[r:r + 8, :]
            keep = (band >= low) & (band < high)
            vals.append(jnp.where(keep, v, MASKED))
        vals = sort16(vals)
        if g:
            vals = merge16([best[t, i] for i in range(16)], vals)
        for i in range(16):
            best[t, i] = vals[i]

    def selects(groups, tiles):
        return [functools.partial(select, g, t) for g in groups for t in tiles]

    def spread(c, dz):
        m = jnp.broadcast_to(lmeta[8 * c + dz], (128, 128)).T
        r = LD * lplace(dz, c)
        lsc[r:r + LD, :] = m[0:LD]
        lband[r:r + LD, :] = m[64:64 + LD]

    def q_first(a, half):
        if half == 0:
            ext_wait(a, 0)
        q_wait(a, 0, half)
        if (a, half) == (1, 1):
            q_send(1, 0, 1, (-1, 0))
        if (a, half) == (3, 0):
            q_send(3, 0, 0, (1, 0))
        q_send(a, 0, half, (0, 1))
        q_send(a, 0, half, (0, -1))

    def q_across(half):
        q_wait(2, 0, half)
        q_send(2, 0, half, (0, 1))
        q_send(2, 0, half, (0, -1))

    def q_second(a, half):
        b = 1 if half else 3
        if a == 0:
            ext_wait(0, b)
        q_wait(a, b, half)
        q_send(a, b, half, (0, -1) if half else (0, 1))

    def q_rest(a):
        q_wait(a, 1, 0)
        q_wait(a, 3, 1)

    q_first(1, 0)
    q_first(3, 0)
    l_forward(1, 0)
    q_first(1, 1)
    m_forward(1)
    l_forward(1, 1)
    q_second(0, 1)
    q_first(3, 1)
    q_across(0)
    sib_forward(1)
    q_second(3, 0)
    q_second(0, 0)
    q_second(1, 0)
    q_across(1)
    q_second(1, 1)
    prepare((0,))
    m_forward(2)
    l_forward(2, 0)
    q_rest(0)
    q_rest(1)
    prepare((1,))
    q_second(3, 1)
    l_forward(2, 1)
    q_second(2, 0)
    sib_forward(2)
    m_forward(3)
    q_second(2, 1)
    sib_wait(0)
    sib_wait(1)
    multiply(0, 288, 0)
    l_last()
    sib_wait(2)
    multiply(288, 192, 0)
    wait_all(qbuf.at[pl.ds(0, 64)], qr_sem.at[37])
    prepare((2,))
    wait_all(qbuf.at[pl.ds(0, 128)], qr_sem.at[36])
    prepare((3,))
    m_wait(4)
    pltpu.make_async_remote_copy(
        src_ref=lmeta.at[pl.ds(0, 8)], dst_ref=lmeta.at[pl.ds(8, 8)], send_sem=left_sem.at[6],
        recv_sem=mr_sem.at[0], device_id=column(0, 1), device_id_type=MESH,
    ).start()
    multiply(0, 288, 1, [functools.partial(spread, 0, dz) for dz in range(8)])
    l_wait(3, 1)
    sib_forward(3)
    l_wait(4, 0)
    sib_forward(4)
    pltpu.make_async_copy(lmeta.at[pl.ds(8, 8)], lmeta.at[pl.ds(8, 8)], mr_sem.at[0]).wait()
    multiply(288, 192, 1, [functools.partial(spread, 1, dz) for dz in range(8)])
    sib_wait(3)
    sib_wait(4)

    def finish(t):
        vals = [best[t, i] for i in range(16)]
        for sh in (4, 2, 1):
            vals = merge16(vals, [pltpu.roll(v, sh, 0) for v in vals])
        for i in range(16):
            fin[t, i:i + 1, :] = vals[i][0:1]
        for p in (3, 2, 1, 0):
            n = 4 * t + p
            if n == 0:
                continue
            a, b = SLOTS[n]
            pltpu.make_async_remote_copy(
                src_ref=fin.at[t], dst_ref=got.at[n], send_sem=f_sem.at[0],
                recv_sem=f_sem.at[1], device_id=plane(a, b), device_id_type=MESH,
            ).start()

    for tiles in ((3, 2), (1, 0)):
        multiply(480, 288, tiles[1] // 2, selects(range(3), tiles))
        for t in tiles:
            for g in range(3, 6):
                select(g, t)
            finish(t)
    got[0] = fin[0]
    wait_all(lbuf.at[pl.ds(0, 7 * LD)], left_sem.at[0])
    wait_all(lmeta.at[pl.ds(0, 7)], left_sem.at[1])
    wait_all(lbuf.at[pl.ds(0, 8 * LD)], left_sem.at[2])
    wait_all(lbuf.at[pl.ds(0, 4 * QD)], left_sem.at[3])
    wait_all(qbuf.at[pl.ds(0, 4 * QD), pl.ds(BINS, 128)], left_sem.at[4])
    wait_all(qbuf.at[pl.ds(0, 11 * QD)], left_sem.at[5])
    wait_all(lmeta.at[pl.ds(0, 8)], left_sem.at[6])
    pltpu.make_async_copy(got.at[pl.ds(1, 15)], got.at[pl.ds(1, 15)], f_sem.at[0]).wait()
    pltpu.make_async_copy(got.at[pl.ds(1, 15)], got.at[pl.ds(1, 15)], f_sem.at[1]).wait()

    part = lax.div(lax.broadcasted_iota(jnp.int32, (8, 128), 1), QD)
    vals = []
    for r in range(16):
        rows = []
        for t in range(4):
            v = got[4 * t, r:r + 1, :]
            for p in range(1, 4):
                v = jnp.where(part[0:1] == p, got[4 * t + p, r:r + 1, :], v)
            rows.append(v)
        vals.append(jnp.concatenate(rows + rows, axis=0))
    for sh in (2, 1):
        vals = merge16(vals, [pltpu.roll(v, sh, 0) for v in vals])
    for sh in (64, 32):
        vals = merge16(vals, [pltpu.roll(v, sh, 1) for v in vals])
    for i in range(TOPK):
        out[i:i + 1, :] = vals[i][0:1, 0:QD]


def local(queries, windows, library, bands, shifts):
    dma = pltpu.SemaphoreType.DMA
    f32, bf16 = jnp.float32, jnp.bfloat16
    hbm = pl.BlockSpec(memory_space=pltpu.HBM)
    return pl.pallas_call(
        kernel,
        out_shape=jax.ShapeDtypeStruct((TOPK, QD), f32),
        in_specs=[hbm] * 5,
        out_specs=pl.BlockSpec(memory_space=pltpu.VMEM),
        scratch_shapes=[
            pltpu.SMEM((2,), jnp.int32),
            pltpu.SMEM((6,), jnp.int32),
            pltpu.SMEM((NOFF,), jnp.int32),
            pltpu.VMEM((NQ, WIDE), bf16),
            pltpu.VMEM((NL, BINS), bf16),
            pltpu.VMEM((4, PAD, 128), f32),
            pltpu.VMEM((NOFF, BINS, NQ), bf16),
            pltpu.VMEM((NL, NQ), f32),
            pltpu.VMEM((NL, 128), f32),
            pltpu.VMEM((NL, 128), f32),
            pltpu.VMEM((8, NQ), f32),
            pltpu.VMEM((4, 16, 8, 128), f32),
            pltpu.VMEM((16, 1, 128), f32),
            pltpu.VMEM((4, 16, 128), f32),
            pltpu.VMEM((16, 16, 128), f32),
            dma((5,)), dma((7,)), dma((38,)), dma((9,)), dma((5,)), dma((5,)), dma((2,)),
        ],
        compiler_params=pltpu.CompilerParams(
            collective_id=0, has_side_effects=True, vmem_limit_bytes=62 * 2**20
        ),
        cost_estimate=pl.CostEstimate(
            flops=2 * NQ * NL * BINS * NOFF, bytes_accessed=2 * (QD + LD) * BINS, transcendentals=0
        ),
    )(queries, windows, library, bands, shifts).T


def solution(mesh):
    return jax.shard_map(
        local,
        mesh=mesh,
        in_specs=(
            P(("blk", "grp"), None),
            P(("blk", "grp")),
            P(("blk", "grp"), None),
            P(("blk", "grp")),
            P(),
        ),
        out_specs=P(("blk", "grp"), None),
        check_vma=False,
    )
```
